512 devices in a mesh: tm: 8 (over z_lo), rows: 64 (over z_hi, y, x, core).
Axes of the slice: x: 4, y: 4, z: 16 (z_hi: 2, z_lo: 8; z = z_hi * 8 + z_lo), core: 2. Of those that a mesh axis runs over, the one named last changes fastest.
Arguments:
- frames_in: bfloat16 [64, 128, 32, 192], P('tm', 'rows'), may hold values from -6 to 6
- slot_frame: int32 [64], P('tm'), may hold values from 0 to 63, as said below
- shot_spans: int32 [4], replicated, may hold values from 1 to 8, 16 in all
- gain_one: float32 [192], replicated, may hold values from 0.5 to 1.5
- conv_one: bfloat16 [3, 3, 3, 192, 192], replicated, may hold values from -0.078125 to 0.078125
- bias_one: float32 [192], replicated, may hold values from -3 to 3
- gain_two: float32 [192], replicated, may hold values from 0.5 to 1.5
- conv_two: bfloat16 [3, 3, 3, 192, 192], replicated, may hold values from -0.078125 to 0.078125
- bias_two: float32 [192], replicated, may hold values from -3 to 3
Outputs:
- encoded: bfloat16 [64, 128, 32, 192], P('tm', 'rows')
The draws below stay inside these ranges and needn't reach their ends.
Inputs may be any that keep to these rules, and one draw needn't show every extreme that they name: `slot_frame`: every frame 0 to 63 is held by exactly one slot; a device's 8 slots hold, for each destination device (frame // 8), either none or exactly 2 of its frames. `shot_spans`: the counts sum to 16; the largest is 8.
All inputs are finite; a program needn't handle non-finite values.
Results may differ from the reference program's by a relative error of at most 0.0035.
Values may be sent and summed in bfloat16 or wider, within the bound.
A program may use at most 64 MiB of HBM per device.

```python
import math
import jax
import jax.numpy as jnp
import numpy as np
from jax import lax

C = 192
SPAN = 4
CAP = 2
SHOTS = 4
COLS = 32
FR_DEV = 8
NCH = 16
NF = 64
ROWS = 128
MOST = 8
BLOCKS = 4
N_TM = 8


def draw_slot_frame(key, part):
    key = jax.random.fold_in(key, 11)
    first_key, second_key, third_key = jax.random.split(key, 3)
    offsets = jax.random.permutation(first_key, N_TM)[:BLOCKS]
    source = jnp.arange(N_TM)[:, None, None]
    block_index = jnp.arange(BLOCKS)[None, :, None]
    within = jnp.arange(CAP)[None, None, :]
    target = (source - offsets[None, :, None]) % N_TM
    local_orders = jax.vmap(lambda one_key: jax.random.permutation(one_key, FR_DEV))(jax.random.split(second_key, N_TM))
    local_place = local_orders[target, block_index * CAP + within]
    framed = (target * FR_DEV + local_place).reshape(N_TM, FR_DEV)
    slot_orders = jax.vmap(lambda one_key: jax.random.permutation(one_key, FR_DEV))(jax.random.split(third_key, N_TM))
    framed = jnp.take_along_axis(framed, slot_orders, axis=1)
    return framed.reshape(-1).astype(jnp.int32)


def levels(stream_key, dims, shards, least, high):
    level = 1.0
    for dim, blocks in shards:
        heights = jax.random.uniform(jax.random.fold_in(jax.random.fold_in(stream_key, 6), dim), (blocks,), jnp.float32, least / len(shards), high / len(shards))
        level = level * jnp.repeat(jnp.exp(heights), dims[dim] // blocks).reshape((-1,) + (1,) * (len(dims) - 1 - dim))
    return level


def profile(number_of, total, bound, lean):
    loads = [(1 << 20) // math.isqrt(rank ** lean) + 1 for rank in range(2, number_of + 1)]
    surplus, holding = total - bound - (number_of - 1), [1] * (number_of - 1)
    while surplus > 0:
        free = [i for i in range(number_of - 1) if holding[i] < bound]
        whole, left = sum([loads[i] for i in free]), surplus
        for i in free:
            more = min(bound - holding[i], max(1, left * loads[i] // whole), surplus)
            holding[i] = holding[i] + more
            surplus = surplus - more
    return np.array([bound] + holding)


def ragged(stream_key, amount, total, limit, skew):
    if amount == 2:
        one = jax.random.randint(stream_key, (), max(1, total - limit), min(limit, total - 1) + 1)
        return jnp.stack([one, total - one])
    tallies = jnp.asarray(profile(amount, total, limit, skew), jnp.int32)
    pairs = (amount - 1) // 2
    source_of, receiver = tallies[1:1 + 2 * pairs:2], tallies[2:2 + 2 * pairs:2]
    slack = jnp.minimum(source_of - 1, limit - receiver)
    moved = jax.random.randint(jax.random.fold_in(stream_key, 1), (pairs,), 0, 1 << 20) % (slack + 1)
    tallies = tallies.at[1:1 + 2 * pairs:2].set(source_of - moved).at[2:2 + 2 * pairs:2].set(receiver + moved)
    return tallies[jax.random.permutation(jax.random.fold_in(stream_key, 2), amount)]


def bell_draw(own_key, dims, width, most, cuts=(), kind=jnp.bfloat16):
    drawn = width * jax.random.normal(own_key, dims, jnp.float32)
    if cuts:
        drawn = drawn * levels(own_key, dims, cuts, -0.22, 0.18)
    return jnp.clip(drawn, -most, most).astype(kind)


def setup_inputs(seed: int = 0) -> dict:
    key_list = jax.random.split(jax.random.key(seed), 10)
    return {
        "frames_in": bell_draw(key_list[0], (NF, ROWS, COLS, C), 1.0, 6.0, ((0, 8), (1, 64))),
        "slot_frame": draw_slot_frame(jax.random.fold_in(key_list[9], 71), 0),
        "shot_spans": ragged(key_list[2], SHOTS, NCH, MOST, 0).astype(jnp.int32),
        "gain_one": jnp.clip(jax.random.uniform(key_list[3], (C,), jnp.float32, 0.5, 1.5), 0.5, 1.5),
        "conv_one": bell_draw(key_list[4], (3, 3, 3, C, C), (27 * C) ** -0.5, 0.078125),
        "bias_one": bell_draw(key_list[5], (C,), 0.5, 3.0, (), jnp.float32),
        "gain_two": jnp.clip(jax.random.uniform(key_list[6], (C,), jnp.float32, 0.5, 1.5), 0.5, 1.5),
        "conv_two": bell_draw(key_list[7], (3, 3, 3, C, C), (27 * C) ** -0.5, 0.078125),
        "bias_two": bell_draw(key_list[8], (C,), 0.5, 3.0, (), jnp.float32),
    }


def norm_silu(values, gain):
    values = values.astype(jnp.float32)
    scaled = values * lax.rsqrt(lax.optimization_barrier(jnp.mean(values * values, axis=-1, keepdims=True)) + 1e-06) * gain
    return jax.nn.silu(scaled)

def causal_conv(frames_all, weight, bias_term, opened):
    frame_count = frames_all.shape[0]
    row_count = frames_all.shape[1]
    col_count = frames_all.shape[2]
    chan_count = frames_all.shape[3]
    padded = jnp.pad(frames_all, ((2, 0), (1, 1), (1, 1), (0, 0)))
    position = jnp.arange(frame_count)
    summed = jnp.zeros((frame_count * row_count * col_count, chan_count), jnp.float32)
    for time_tap in range(3):
        delay = 2 - time_tap
        kept_mask = (position % SPAN >= delay) | jnp.logical_not(opened[position // SPAN])
        shifted = jnp.where(kept_mask[:, None, None, None], padded[time_tap:time_tap + frame_count], jnp.zeros((), frames_all.dtype))
        for row_tap in range(3):
            for col_tap in range(3):
                tile = shifted[:, row_tap:row_tap + row_count, col_tap:col_tap + col_count].reshape(-1, chan_count)
                summed = summed + jnp.dot(tile, weight[time_tap, row_tap, col_tap], preferred_element_type=jnp.float32)
    return summed.reshape(frame_count, row_count, col_count, chan_count) + bias_term

def reference(frames_in, slot_frame, shot_spans, gain_one, conv_one, bias_one, gain_two, conv_two, bias_two):
    video = jnp.zeros_like(frames_in).at[slot_frame].set(frames_in)
    starts = jnp.cumsum(shot_spans) - shot_spans
    opened = jnp.any(starts[None, :] == jnp.arange(NCH)[:, None], axis=1)
    first = norm_silu(video, gain_one).astype(jnp.bfloat16)
    hidden = causal_conv(first, conv_one, bias_one, opened)
    second = norm_silu(hidden, gain_two).astype(jnp.bfloat16)
    branch = causal_conv(second, conv_two, bias_two, opened)
    return (video.astype(jnp.float32) + branch).astype(jnp.bfloat16)
```

```python
import functools

import jax
import jax.numpy as jnp
from jax import lax
from jax.experimental import pallas as pl
from jax.experimental.pallas import tpu as pltpu
from jax.sharding import PartitionSpec as P

SPAN = 4
CH = 192
COLS = 32
N_TM = 8
F = 8
PACK = 48
ORDER = (4, 3, 5, 2, 6, 1, 7)
F32 = jnp.float32
BF16 = jnp.bfloat16
MESH = pl.DeviceIdType.MESH


def remote(src, dst, send, recv, tm, rows):
    return pltpu.make_async_remote_copy(
        src_ref=src, dst_ref=dst, send_sem=send, recv_sem=recv, device_id=(tm, rows), device_id_type=MESH
    )


def silu(u):
    return u / (1.0 + jnp.exp(-u))


def spread(packed):
    low, pairs = packed[:COLS], packed[COLS:]
    high = jnp.concatenate([pairs[:, :64], pairs[:, 64:]], axis=0)
    return jnp.concatenate([low, high], axis=1)


def gathered(image_row):
    high = image_row[:, 128:]
    pairs = jnp.concatenate([high[:16], high[16:]], axis=1)
    return jnp.concatenate([image_row[:, :128], pairs], axis=0)


def norm_packed(packed, gain_low, gain_pairs):
    low, pairs = packed[:COLS], packed[COLS:]
    left = lax.broadcasted_iota(jnp.int32, pairs.shape, 1) < 64
    low_sum = jnp.sum(low * low, axis=-1, keepdims=True)
    squares = pairs * pairs
    left_sum = jnp.sum(jnp.where(left, squares, 0.0), axis=-1, keepdims=True)
    both_sum = jnp.sum(squares, axis=-1, keepdims=True)
    total = low_sum + jnp.concatenate([left_sum, both_sum - left_sum], axis=0)
    scale = lax.rsqrt(total * (1.0 / CH) + 1e-06)
    low_out = silu(low * scale * gain_low)
    pairs_out = silu(pairs * jnp.where(left, scale[:16], scale[16:]) * gain_pairs)
    return low_out, pairs_out


def col_taps(left, middle, right):
    count = middle.shape[0]
    col = lax.broadcasted_iota(jnp.int32, middle.shape, 0) % COLS
    from_left = jnp.where(col == 0, 0.0, pltpu.roll(left, 1, 0))
    from_right = jnp.where(col == COLS - 1, 0.0, pltpu.roll(right, count - 1, 0))
    return middle + from_left + from_right


def conv(source, base, frames, rows, weight):
    count = frames * rows * COLS
    sums = [jnp.zeros((count, CH), F32) for _ in range(3)]
    for time_tap in range(3):
        for row_tap in range(3):
            tile = source[pl.ds(base + time_tap, frames), pl.ds(row_tap, rows)].reshape(count, CH)
            for col_tap in range(3):
                tap = weight[(time_tap * 3 + row_tap) * 3 + col_tap]
                sums[col_tap] = sums[col_tap] + jnp.dot(tile, tap, preferred_element_type=F32)
    return col_taps(*sums)


def kernel(
    n_rows,
    frames, slots, slots_v, spans, gain_low, gain_pairs, gain_two, bias_one, bias_two, conv_one, conv_two,
    out,
    w_one, w_two, packed, outgoing, arrived, labels, labels_s, video, own, up, down, before, before_up, before_down,
    grid_one, grid_two,
    w_sem, label_sem, a_send, a_recv, l_send, l_recv, h_send, h_recv,
):
    me = lax.axis_index("tm")
    row = lax.axis_index("rows")
    has_up, has_down = row > 0, row < n_rows - 1
    has_next, has_before = me < N_TM - 1, me > 0

    load_one = pltpu.make_async_copy(conv_one, w_one, w_sem.at[0])
    load_two = pltpu.make_async_copy(conv_two, w_two, w_sem.at[1])
    load_one.start()
    load_two.start()

    barrier = pltpu.get_barrier_semaphore()
    for step in range(1, N_TM):
        pl.semaphore_signal(barrier, inc=1, device_id=(lax.rem(me + step, N_TM), row), device_id_type=MESH)
    peers = jnp.int32(N_TM - 1)
    for has_row, row_step in ((has_up, -1), (has_down, 1)):
        for has_tm, tm_step in ((None, 0), (has_next, 1), (has_before, -1)):
            there = has_row if has_tm is None else jnp.logical_and(has_row, has_tm)
            peers = peers + there.astype(jnp.int32)

            @pl.when(there)
            def _():
                pl.semaphore_signal(
                    barrier, inc=1, device_id=(me + tm_step, row + row_step), device_id_type=MESH
                )

    for slot in range(F):
        for line in range(2):
            packed[slot, line * PACK : (line + 1) * PACK] = gathered(frames[slot, line])
    for step in range(N_TM):
        target = lax.rem(me + step, N_TM)
        count = jnp.int32(0)
        picks = [jnp.int32(0), jnp.int32(0)]
        for slot in range(F):
            mine = lax.shift_right_logical(slots[slot], 3) == target
            for rank in range(2):
                picks[rank] = jnp.where(jnp.logical_and(mine, count == rank), slot, picks[rank])
            count = count + mine.astype(jnp.int32)
        for rank in range(2):
            block = packed[picks[rank]]
            if step:
                outgoing[2 * step + rank] = block
            else:
                arrived[rank] = block

    pl.semaphore_wait(barrier, peers)

    label_copies, frame_copies = {}, {}
    for step in ORDER:
        label_copies[step] = remote(
            slots_v.at[pl.ds(0, 1)], labels.at[pl.ds(step, 1)], l_send.at[step], l_recv.at[step],
            lax.rem(me + step, N_TM), row,
        )
        label_copies[step].start()
    for step in ORDER:
        frame_copies[step] = remote(
            outgoing.at[pl.ds(2 * step, 2)], arrived.at[pl.ds(2 * step, 2)], a_send.at[step], a_recv.at[step],
            lax.rem(me + step, N_TM), row,
        )
        frame_copies[step].start()

    @pl.when(jnp.logical_not(has_up))
    def _():
        up[...] = jnp.zeros_like(up)
        before_up[...] = jnp.zeros_like(before_up)

    @pl.when(jnp.logical_not(has_down))
    def _():
        down[...] = jnp.zeros_like(down)
        before_down[...] = jnp.zeros_like(before_down)

    @pl.when(jnp.logical_not(has_before))
    def _():
        before[...] = jnp.zeros_like(before)
        before_up[...] = jnp.zeros_like(before_up)
        before_down[...] = jnp.zeros_like(before_down)

    labels[0:1] = slots_v[0:1]
    for step in ORDER:
        label_copies[step].wait()
    to_scalars = pltpu.make_async_copy(labels, labels_s, label_sem)
    to_scalars.start()
    to_scalars.wait()

    def scan_source(step, places):
        count = jnp.int32(0)
        for slot in range(F):
            held = labels_s[step, slot]
            mine = lax.shift_right_logical(held, 3) == me
            local = jnp.bitwise_and(held, F - 1)
            places = tuple(
                jnp.where(jnp.logical_and(mine, local == f), 2 * step + jnp.minimum(count, 1), places[f]) for f in range(F)
            )
            count = count + mine.astype(jnp.int32)
        return places

    places = lax.fori_loop(0, N_TM, scan_source, (jnp.int32(0),) * F)

    opened = []
    for span in range(2):
        start, hit = jnp.int32(0), jnp.bool_(False)
        for shot in range(4):
            hit = jnp.logical_or(hit, start == 2 * me + span)
            start = start + spans[shot]
        opened.append(hit)
    keep = [jnp.where(hit, 0.0, 1.0).astype(BF16) for hit in opened]

    for step in ORDER:
        frame_copies[step].wait()

    for f in range(F):
        block = arrived[places[f]]
        for line in range(2):
            part = block[line * PACK : (line + 1) * PACK]
            video[f, line] = spread(part)
            low, pairs = norm_packed(part.astype(F32), gain_low[...], gain_pairs[...])
            own[f, line * PACK : line * PACK + COLS] = low.astype(BF16)
            own[f, line * PACK + COLS : (line + 1) * PACK] = pairs.astype(BF16)

    last = pl.ds(F - SPAN, SPAN)
    sends = (
        (has_up, own, down, 0, 0, -1),
        (has_down, own, up, 1, 0, 1),
        (jnp.logical_and(has_next, has_up), own.at[last], before_down, 2, 1, -1),
        (jnp.logical_and(has_next, has_down), own.at[last], before_up, 3, 1, 1),
        (has_next, own.at[last], before, 4, 1, 0),
    )
    arrivals = (has_down, has_up, jnp.logical_and(has_before, has_down), jnp.logical_and(has_before, has_up), has_before)
    halos = [
        remote(src, dst, h_send.at[i], h_recv.at[i], me + tm_step, row + row_step)
        for _, src, dst, i, tm_step, row_step in sends
    ]
    for (there, *_), copy in zip(sends, halos):

        @pl.when(there)
        def _():
            copy.start()

    def place(f, lines, base, source, keep_one):
        for line in range(2):
            value = spread(source[lines, line * PACK : (line + 1) * PACK])
            grid_one[(8 if f >= SPAN else 6) + f, base + line] = value
            if f in (2, 3):
                grid_one[8 + f, base + line] = jnp.where(opened[1], jnp.zeros_like(value), value)

    def place_before(f, base, source):
        for line in range(2):
            value = spread(source[f, line * PACK : (line + 1) * PACK])
            grid_one[f, base + line] = value
            if f in (2, 3):
                grid_one[2 + f, base + line] = jnp.where(opened[0], jnp.zeros_like(value), value)

    for f in range(F):
        place(f, f, 2, own, keep)

    for there, copy in zip(arrivals, halos):

        @pl.when(there)
        def _():
            copy.wait_recv()

    for f in range(F):
        place(f, f, 0, up, keep)
        place(f, f, 4, down, keep)
    for f in range(SPAN):
        place_before(f, 2, before)
        place_before(f, 0, before_up)
        place_before(f, 4, before_down)

    load_one.wait()

    line_of = lax.broadcasted_iota(jnp.int32, (2 * 4 * COLS, 1), 0) // COLS % 4
    outside = jnp.logical_or(
        jnp.logical_and(line_of == 0, jnp.logical_not(has_up)),
        jnp.logical_and(line_of == 3, jnp.logical_not(has_down)),
    )
    for pair, base in enumerate((0, 4, 6, 10, 12)):
        hidden = conv(grid_one, base, 2, 4, w_one) + bias_one[...]
        mean = jnp.sum(hidden * hidden, axis=-1, keepdims=True) * (1.0 / CH)
        second = silu(hidden * lax.rsqrt(mean + 1e-06) * gain_two[...])
        second = jnp.where(outside, 0.0, second).astype(BF16).reshape(2, 4, COLS, CH)
        if pair == 0:
            grid_two[0:2] = jnp.where(opened[0], jnp.zeros_like(second), second)
        else:
            at = 2 * pair if pair < 3 else 2 * pair + 2
            grid_two[at : at + 2] = second
            if pair == 2:
                grid_two[6:8] = jnp.where(opened[1], jnp.zeros_like(second), second)

    load_two.wait()
    for span in range(2):
        branch = conv(grid_two, 6 * span, SPAN, 2, w_two) + bias_two[...]
        held = video[SPAN * span : SPAN * (span + 1)].astype(F32)
        out[SPAN * span : SPAN * (span + 1)] = (held + branch.reshape(SPAN, 2, COLS, CH)).astype(BF16)

    for (there, *_), copy in zip(sends, halos):

        @pl.when(there)
        def _():
            copy.wait_send()


def body(
    frames_in, slot_frame, shot_spans, gain_one, conv_one, bias_one, gain_two, conv_two, bias_two
):
    slots_v = jnp.broadcast_to(jnp.pad(slot_frame, (0, 128 - F))[None, :], (8, 128))
    gain_low = gain_one[None, :128]
    gain_pairs = jnp.concatenate([gain_one[128:], gain_one[128:]])[None, :]
    vmem = pl.BlockSpec(memory_space=pltpu.VMEM)
    smem = pl.BlockSpec(memory_space=pltpu.SMEM)
    hbm = pl.BlockSpec(memory_space=pl.ANY)
    dma = pltpu.SemaphoreType.DMA
    taps = (27, CH, CH)
    whole, tail = (F, 2 * PACK, 128), (SPAN, 2 * PACK, 128)
    return pl.pallas_call(
        functools.partial(kernel, lax.axis_size("rows")),
        out_shape=jax.ShapeDtypeStruct(frames_in.shape, BF16),
        in_specs=[vmem, smem, vmem, smem, vmem, vmem, vmem, vmem, vmem, hbm, hbm],
        out_specs=vmem,
        scratch_shapes=[
            pltpu.VMEM(taps, BF16),
            pltpu.VMEM(taps, BF16),
            pltpu.VMEM(whole, BF16),
            pltpu.VMEM((2 * N_TM, 2 * PACK, 128), BF16),
            pltpu.VMEM((2 * N_TM, 2 * PACK, 128), BF16),
            pltpu.VMEM((8, 128), jnp.int32),
            pltpu.SMEM((8, 128), jnp.int32),
            pltpu.VMEM((F, 2, COLS, CH), BF16),
            pltpu.VMEM(whole, BF16),
            pltpu.VMEM(whole, BF16),
            pltpu.VMEM(whole, BF16),
            pltpu.VMEM(tail, BF16),
            pltpu.VMEM(tail, BF16),
            pltpu.VMEM(tail, BF16),
            pltpu.VMEM((16, 6, COLS, CH), BF16),
            pltpu.VMEM((12, 4, COLS, CH), BF16),
            dma((2,)),
            dma,
            dma((N_TM,)),
            dma((N_TM,)),
            dma((N_TM,)),
            dma((N_TM,)),
            dma((5,)),
            dma((5,)),
        ],
        name="residual_block",
        compiler_params=pltpu.CompilerParams(
            collective_id=1, has_side_effects=True, vmem_limit_bytes=40 << 20
        ),
    )(
        frames_in, slot_frame, slots_v, shot_spans, gain_low, gain_pairs, gain_two[None, :],
        bias_one[None, :], bias_two[None, :], conv_one.reshape(taps), conv_two.reshape(taps),
    )


def solution(mesh):
    placed = (P("tm", "rows", None, None), P("tm"), P(), P(), P(), P(), P(), P(), P())
    return jax.shard_map(
        body, mesh=mesh, in_specs=placed, out_specs=P("tm", "rows", None, None), check_vma=False
    )
```

```python
import functools

import jax
import jax.numpy as jnp
from jax import lax
from jax.experimental import pallas as pl
from jax.experimental.pallas import tpu as pltpu
from jax.sharding import PartitionSpec as P

SPAN = 4
CH = 192
COLS = 32
N_TM = 8
F = 8
PACK = 48
ORDER = (4, 3, 5, 2, 6, 1, 7)
F32 = jnp.float32
BF16 = jnp.bfloat16
MESH = pl.DeviceIdType.MESH


def remote(src, dst, send, recv, tm, rows):
    return pltpu.make_async_remote_copy(
        src_ref=src, dst_ref=dst, send_sem=send, recv_sem=recv, device_id=(tm, rows), device_id_type=MESH
    )


def silu(u):
    return u / (1.0 + jnp.exp(-u))


def spread(packed):
    low, pairs = packed[:COLS], packed[COLS:]
    high = jnp.concatenate([pairs[:, :64], pairs[:, 64:]], axis=0)
    return jnp.concatenate([low, high], axis=1)


def gathered(image_row):
    high = image_row[:, 128:]
    pairs = jnp.concatenate([high[:16], high[16:]], axis=1)
    return jnp.concatenate([image_row[:, :128], pairs], axis=0)


def norm_packed(packed, gain_low, gain_pairs):
    values = packed.astype(F32)
    low, pairs = values[:COLS], values[COLS:]
    left = lax.broadcasted_iota(jnp.int32, pairs.shape, 1) < 64
    low_sum = jnp.sum(low * low, axis=-1, keepdims=True)
    squares = pairs * pairs
    left_sum = jnp.sum(jnp.where(left, squares, 0.0), axis=-1, keepdims=True)
    right_sum = jnp.sum(jnp.where(left, 0.0, squares), axis=-1, keepdims=True)
    total = low_sum + jnp.concatenate([left_sum, right_sum], axis=0)
    scale = lax.rsqrt(total * (1.0 / CH) + 1e-06)
    low_out = silu(low * scale * gain_low)
    pairs_out = silu(pairs * jnp.where(left, scale[:16], scale[16:]) * gain_pairs)
    return jnp.concatenate([low_out.astype(BF16), pairs_out.astype(BF16)], axis=0)


def col_taps(left, middle, right):
    count = middle.shape[0]
    col = lax.broadcasted_iota(jnp.int32, middle.shape, 0) % COLS
    from_left = jnp.where(col == 0, 0.0, pltpu.roll(left, 1, 0))
    from_right = jnp.where(col == COLS - 1, 0.0, pltpu.roll(right, count - 1, 0))
    return middle + from_left + from_right


def conv(source, base, frames, rows, weight):
    count = frames * rows * COLS
    sums = [jnp.zeros((count, CH), F32) for _ in range(3)]
    for time_tap in range(3):
        for row_tap in range(3):
            tile = source[pl.ds(base + time_tap, frames), pl.ds(row_tap, rows)].reshape(count, CH)
            for col_tap in range(3):
                tap = weight[(time_tap * 3 + row_tap) * 3 + col_tap]
                sums[col_tap] = sums[col_tap] + jnp.dot(tile, tap, preferred_element_type=F32)
    return col_taps(*sums)


def kernel(
    n_rows,
    frames_h, slots, spans, gain_one, conv_one_h, bias_one, gain_two, conv_two_h, bias_two,
    out,
    frames, w_one, w_two,
    packed, packed_first, outgoing, outgoing_first, arrived, first, up_first, down_first,
    labels, labels_s, tail, tail_before, second_tail, second_before, grid_one, grid_two,
    in_sem, label_sem, l_send, l_recv, a_send, a_recv, up_send, up_recv, down_send, down_recv,
    t_send, t_recv, s_send, s_recv,
):
    me = lax.axis_index("tm")
    row = lax.axis_index("rows")
    has_up, has_down = row > 0, row < n_rows - 1
    has_next, has_before = me < N_TM - 1, me > 0
    far_up, far_down = row == n_rows, row == n_rows
    near_up = jnp.logical_and(has_up, jnp.logical_not(far_up))
    near_down = jnp.logical_and(has_down, jnp.logical_not(far_down))

    loads = [
        pltpu.make_async_copy(src, dst, in_sem.at[i])
        for i, (src, dst) in enumerate((
            (frames_h, frames), (conv_one_h, w_one), (conv_two_h, w_two),
        ))
    ]
    for load in loads:
        load.start()

    barrier = pltpu.get_barrier_semaphore()
    for step in range(1, N_TM):
        pl.semaphore_signal(barrier, inc=1, device_id=(lax.rem(me + step, N_TM), row), device_id_type=MESH)
    peers = jnp.int32(N_TM - 1)
    for near, far, row_step in ((near_up, far_up, -1), (near_down, far_down, 1)):
        peers = peers + near.astype(jnp.int32) + N_TM * far.astype(jnp.int32)

        @pl.when(near)
        def _():
            pl.semaphore_signal(barrier, inc=1, device_id=(me, row + row_step), device_id_type=MESH)

        @pl.when(far)
        def _():
            for tm in range(N_TM):
                pl.semaphore_signal(barrier, inc=1, device_id=(tm, row + row_step), device_id_type=MESH)

    lane = lax.broadcasted_iota(jnp.int32, (1, 128), 1)
    held = jnp.zeros((1, 128), jnp.int32)
    for slot in range(F):
        held = jnp.where(lane == slot, slots[slot], held)
    labels[0:1] = held

    loads[0].wait()
    gain = gain_one[...]
    gain_low = gain[:, :128]
    gain_pairs = jnp.concatenate([gain[:, 128:], gain[:, 128:]], axis=1)
    for slot in range(F):
        for line in range(2):
            span_of = slice(line * PACK, (line + 1) * PACK)
            block = gathered(frames[slot, line])
            packed[slot, span_of] = block
            packed_first[slot, span_of] = norm_packed(block, gain_low, gain_pairs)
    for step in range(N_TM):
        target = lax.rem(me + step, N_TM)
        count = jnp.int32(0)
        picks = [jnp.int32(0), jnp.int32(0)]
        for slot in range(F):
            mine = lax.shift_right_logical(slots[slot], 3) == target
            for rank in range(2):
                picks[rank] = jnp.where(jnp.logical_and(mine, count == rank), slot, picks[rank])
            count = count + mine.astype(jnp.int32)
        for rank in range(2):
            at = 2 * step + rank
            outgoing_first[at] = packed_first[picks[rank]]
            if step:
                outgoing[at] = packed[picks[rank]]
            else:
                arrived[rank] = packed[picks[rank]]
                first[rank] = packed_first[picks[rank]]

    pl.semaphore_wait(barrier, peers)

    def pair_of(ref, step):
        return ref.at[pl.ds(2 * step, 2)]

    label_copies, frame_copies, up_near, up_far, down_near, down_far = {}, {}, {}, {}, {}, {}
    for step in range(N_TM):
        target = lax.rem(me + step, N_TM)
        if step:
            label_copies[step] = remote(
                labels.at[pl.ds(0, 1)], labels.at[pl.ds(step, 1)], l_send.at[step], l_recv.at[step], target, row
            )
            frame_copies[step] = remote(
                pair_of(outgoing, step), pair_of(arrived, step), a_send.at[step], a_recv.at[step], target, row
            )
        up_near[step] = remote(
            pair_of(first, step), pair_of(down_first, step), up_send.at[step], up_recv.at[step], me, row - 1
        )
        down_near[step] = remote(
            pair_of(first, step), pair_of(up_first, step), down_send.at[step], down_recv.at[step], me, row + 1
        )
        up_far[step] = remote(
            pair_of(outgoing_first, step), pair_of(down_first, step), up_send.at[step], up_recv.at[step],
            target, row - 1,
        )
        down_far[step] = remote(
            pair_of(outgoing_first, step), pair_of(up_first, step), down_send.at[step], down_recv.at[step],
            target, row + 1,
        )

    def forward(step):
        @pl.when(near_up)
        def _():
            up_near[step].start()

        @pl.when(near_down)
        def _():
            down_near[step].start()

    for step in ORDER:
        label_copies[step].start()
    for step in ORDER:
        frame_copies[step].start()
    for far, copies in ((far_up, up_far), (far_down, down_far)):

        @pl.when(far)
        def _():
            for step in ORDER + (0,):
                copies[step].start()

    forward(0)

    @pl.when(jnp.logical_not(has_up))
    def _():
        up_first[...] = jnp.zeros_like(up_first)

    @pl.when(jnp.logical_not(has_down))
    def _():
        down_first[...] = jnp.zeros_like(down_first)

    @pl.when(jnp.logical_not(has_before))
    def _():
        tail_before[...] = jnp.zeros_like(tail_before)
        second_before[...] = jnp.zeros_like(second_before)

    for step in ORDER:
        label_copies[step].wait_recv()
    to_scalars = pltpu.make_async_copy(labels, labels_s, label_sem)
    to_scalars.start()
    to_scalars.wait()

    def scan_source(step, places):
        count = jnp.int32(0)
        for slot in range(F):
            held = labels_s[step, slot]
            mine = lax.shift_right_logical(held, 3) == me
            local = jnp.bitwise_and(held, F - 1)
            at = 2 * step + jnp.minimum(count, 1)
            places = tuple(jnp.where(jnp.logical_and(mine, local == f), at, places[f]) for f in range(F))
            count = count + mine.astype(jnp.int32)
        return places

    places = lax.fori_loop(0, N_TM, scan_source, (jnp.int32(0),) * F)

    opened = []
    for span in range(2):
        start, hit = jnp.int32(0), jnp.bool_(False)
        for shot in range(4):
            hit = jnp.logical_or(hit, start == 2 * me + span)
            start = start + spans[shot]
        opened.append(hit)

    for step in ORDER:
        frame_copies[step].wait_recv()
        for rank in range(2):
            for line in range(2):
                span_of = slice(line * PACK, (line + 1) * PACK)
                first[2 * step + rank, span_of] = norm_packed(
                    arrived[2 * step + rank, span_of], gain_low, gain_pairs
                )
        forward(step)

    def tail_copy(side):
        return remote(tail.at[side], tail_before.at[side], t_send.at[side], t_recv.at[side], me + 1, row)

    for k in range(2):
        tail[0, k] = first[places[F - 2 + k]]

    @pl.when(has_next)
    def _():
        tail_copy(0).start()

    for has_side, copies in ((has_down, up_near), (has_up, down_near)):

        @pl.when(has_side)
        def _():
            for step in (0,) + ORDER:
                copies[step].wait_recv()

    for k in range(2):
        tail[1, k] = up_first[places[F - 2 + k]]
        tail[2, k] = down_first[places[F - 2 + k]]

    @pl.when(has_next)
    def _():
        tail_copy(1).start()
        tail_copy(2).start()

    def place(f):
        for source, base in ((first, 2), (up_first, 0), (down_first, 4)):
            block = source[places[f]]
            for line in range(2):
                value = spread(block[line * PACK : (line + 1) * PACK])
                grid_one[(2 if f < SPAN else 4) + f, base + line] = value
                if f in (2, 3):
                    grid_one[4 + f, base + line] = jnp.where(opened[1], jnp.zeros_like(value), value)

    line_of = lax.broadcasted_iota(jnp.int32, (2 * 4 * COLS, 1), 0) // COLS % 4
    outside = jnp.logical_or(
        jnp.logical_and(line_of == 0, jnp.logical_not(has_up)),
        jnp.logical_and(line_of == 3, jnp.logical_not(has_down)),
    )

    def second_of(base):
        hidden = conv(grid_one, base, 2, 4, w_one) + bias_one[...]
        mean = jnp.sum(hidden * hidden, axis=-1, keepdims=True) * (1.0 / CH)
        second = silu(hidden * lax.rsqrt(mean + 1e-06) * gain_two[...])
        second = jnp.where(outside, 0.0, second).astype(BF16).reshape(2, 4, COLS, CH)
        grid_two[base + 2 : base + 4] = second
        return second

    def finish(span):
        branch = conv(grid_two, 6 * span, SPAN, 2, w_two) + bias_two[...]
        for f in range(SPAN):
            block = arrived[places[SPAN * span + f]]
            for line in range(2):
                held = spread(block[line * PACK : (line + 1) * PACK]).astype(F32)
                at = (2 * f + line) * COLS
                out[SPAN * span + f, line] = (held + branch[at : at + COLS]).astype(BF16)

    for f in (4, 5, 6, 7):
        place(f)
    loads[1].wait()
    second = second_of(8)
    for k in range(2):
        for line in range(4):
            second_tail[k, line * PACK : (line + 1) * PACK] = gathered(second[k, line])
    send_second = remote(second_tail, second_before, s_send, s_recv, me + 1, row)

    @pl.when(has_next)
    def _():
        send_second.start()

    for f in (2, 3):
        place(f)
    second_of(6)
    for f in (0, 1):
        place(f)
    second = second_of(2)
    grid_two[6:8] = jnp.where(opened[1], jnp.zeros_like(second), second)
    loads[2].wait()
    finish(1)

    @pl.when(has_before)
    def _():
        for side in range(3):
            tail_copy(side).wait_recv()

    for side, base in ((0, 2), (1, 0), (2, 4)):
        for k in range(2):
            for line in range(2):
                value = spread(tail_before[side, k, line * PACK : (line + 1) * PACK])
                grid_one[k, base + line] = jnp.where(opened[0], jnp.zeros_like(value), value)
    second_of(0)

    @pl.when(has_before)
    def _():
        send_second.wait_recv()

    for k in range(2):
        for line in range(4):
            value = spread(second_before[k, line * PACK : (line + 1) * PACK])
            grid_two[k, line] = jnp.where(opened[0], jnp.zeros_like(value), value)
    finish(0)

    for step in ORDER:
        label_copies[step].wait_send()
        frame_copies[step].wait_send()
    for has_side, copies in ((has_up, up_near), (has_down, down_near)):

        @pl.when(has_side)
        def _():
            for step in (0,) + ORDER:
                copies[step].wait_send()

    @pl.when(has_next)
    def _():
        for side in range(3):
            tail_copy(side).wait_send()
        send_second.wait_send()


def body(
    frames_in, slot_frame, shot_spans, gain_one, conv_one, bias_one, gain_two, conv_two, bias_two
):
    vmem, smem, dma = pltpu.VMEM, pltpu.SMEM, pltpu.SemaphoreType.DMA
    whole = pl.BlockSpec(memory_space=vmem)
    hbm, scalars = pl.BlockSpec(memory_space=pl.ANY), pl.BlockSpec(memory_space=smem)
    taps, vector = (27, CH, CH), (1, CH)
    blocks = vmem((2 * N_TM, 2 * PACK, 128), BF16)
    return pl.pallas_call(
        functools.partial(kernel, lax.axis_size("rows")),
        out_shape=jax.ShapeDtypeStruct(frames_in.shape, BF16),
        in_specs=[hbm, scalars, scalars, whole, hbm, whole, whole, hbm, whole],
        out_specs=whole,
        scratch_shapes=[
            vmem(frames_in.shape, BF16),
            vmem(taps, BF16),
            vmem(taps, BF16),
            vmem((F, 2 * PACK, 128), BF16),
            vmem((F, 2 * PACK, 128), BF16),
            blocks, blocks, blocks, blocks, blocks, blocks,
            vmem((N_TM, 128), jnp.int32),
            smem((N_TM, 128), jnp.int32),
            vmem((3, 2, 2 * PACK, 128), BF16),
            vmem((3, 2, 2 * PACK, 128), BF16),
            vmem((2, 4 * PACK, 128), BF16),
            vmem((2, 4 * PACK, 128), BF16),
            vmem((12, 6, COLS, CH), BF16),
            vmem((12, 4, COLS, CH), BF16),
            dma((3,)),
            dma,
            dma((N_TM,)), dma((N_TM,)),
            dma((N_TM,)), dma((N_TM,)),
            dma((N_TM,)), dma((N_TM,)),
            dma((N_TM,)), dma((N_TM,)),
            dma((3,)), dma((3,)),
            dma, dma,
        ],
        name="residual_block",
        compiler_params=pltpu.CompilerParams(
            collective_id=1, has_side_effects=True, vmem_limit_bytes=60 << 20
        ),
    )(
        frames_in, slot_frame, shot_spans, gain_one.reshape(vector),
        conv_one.reshape(taps), bias_one.reshape(vector), gain_two.reshape(vector),
        conv_two.reshape(taps), bias_two.reshape(vector),
    )


def solution(mesh):
    placed = (P("tm", "rows", None, None), P("tm"), P(), P(), P(), P(), P(), P(), P())
    return jax.shard_map(
        body, mesh=mesh, in_specs=placed, out_specs=P("tm", "rows", None, None), check_vma=False
    )
```

```python
import functools

import jax
import jax.numpy as jnp
from jax import lax
from jax.experimental import pallas as pl
from jax.experimental.pallas import tpu as pltpu
from jax.sharding import PartitionSpec as P

SPAN = 4
CH = 192
COLS = 32
N_TM = 8
F = 8
PACK = 48
ORDER = (4, 3, 5, 2, 6, 1, 7)
F32 = jnp.float32
BF16 = jnp.bfloat16
MESH = pl.DeviceIdType.MESH


def remote(src, dst, send, recv, tm, rows):
    return pltpu.make_async_remote_copy(
        src_ref=src, dst_ref=dst, send_sem=send, recv_sem=recv, device_id=(tm, rows), device_id_type=MESH
    )


def silu(u):
    return u / (1.0 + jnp.exp(-u))


def spread(packed):
    low, pairs = packed[:COLS], packed[COLS:]
    high = jnp.concatenate([pairs[:, :64], pairs[:, 64:]], axis=0)
    return jnp.concatenate([low, high], axis=1)


def gathered(image_row):
    high = image_row[:, 128:]
    pairs = jnp.concatenate([high[:16], high[16:]], axis=1)
    return jnp.concatenate([image_row[:, :128], pairs], axis=0)


def norm_packed(packed, gain_low, gain_pairs):
    values = packed.astype(F32)
    low, pairs = values[:COLS], values[COLS:]
    left = lax.broadcasted_iota(jnp.int32, pairs.shape, 1) < 64
    low_sum = jnp.sum(low * low, axis=-1, keepdims=True)
    squares = pairs * pairs
    left_sum = jnp.sum(jnp.where(left, squares, 0.0), axis=-1, keepdims=True)
    right_sum = jnp.sum(jnp.where(left, 0.0, squares), axis=-1, keepdims=True)
    total = low_sum + jnp.concatenate([left_sum, right_sum], axis=0)
    scale = lax.rsqrt(total * (1.0 / CH) + 1e-06)
    low_out = silu(low * scale * gain_low)
    pairs_out = silu(pairs * jnp.where(left, scale[:16], scale[16:]) * gain_pairs)
    return jnp.concatenate([low_out.astype(BF16), pairs_out.astype(BF16)], axis=0)


def col_taps(left, middle, right):
    count = middle.shape[0]
    col = lax.broadcasted_iota(jnp.int32, middle.shape, 0) % COLS
    from_left = jnp.where(col == 0, 0.0, pltpu.roll(left, 1, 0))
    from_right = jnp.where(col == COLS - 1, 0.0, pltpu.roll(right, count - 1, 0))
    return middle + from_left + from_right


def conv(source, base, frames, rows, weight):
    count = frames * rows * COLS
    sums = [jnp.zeros((count, CH), F32) for _ in range(3)]
    for time_tap in range(3):
        for row_tap in range(3):
            tile = source[pl.ds(base + time_tap, frames), pl.ds(row_tap, rows)].reshape(count, CH)
            for col_tap in range(3):
                tap = weight[(time_tap * 3 + row_tap) * 3 + col_tap]
                sums[col_tap] = sums[col_tap] + jnp.dot(tile, tap, preferred_element_type=F32)
    return col_taps(*sums)


def kernel(
    n_rows,
    frames_h, slots, spans, gain_one, conv_one_h, bias_one, gain_two, conv_two_h, bias_two,
    out,
    frames, w_one, w_two,
    packed, packed_first, outgoing, outgoing_first, arrived, first, up_first, down_first,
    labels, labels_s, tail, tail_before, second_tail, second_before, grid_one, grid_two,
    in_sem, label_sem, l_send, l_recv, a_send, a_recv, up_send, up_recv, down_send, down_recv,
    t_send, t_recv, s_send, s_recv,
):
    me = lax.axis_index("tm")
    row = lax.axis_index("rows")
    has_up, has_down = row > 0, row < n_rows - 1
    has_next, has_before = me < N_TM - 1, me > 0
    far_up, far_down = row == n_rows // 2, row == n_rows // 2 - 1
    near_up = jnp.logical_and(has_up, jnp.logical_not(far_up))
    near_down = jnp.logical_and(has_down, jnp.logical_not(far_down))

    loads = [
        pltpu.make_async_copy(src, dst, in_sem.at[i])
        for i, (src, dst) in enumerate((
            (frames_h, frames), (conv_one_h, w_one), (conv_two_h, w_two),
        ))
    ]
    for load in loads:
        load.start()

    barrier = pltpu.get_barrier_semaphore()
    for step in range(1, N_TM):
        pl.semaphore_signal(barrier, inc=1, device_id=(lax.rem(me + step, N_TM), row), device_id_type=MESH)
    peers = jnp.int32(N_TM - 1)
    for near, far, row_step in ((near_up, far_up, -1), (near_down, far_down, 1)):
        peers = peers + near.astype(jnp.int32) + N_TM * far.astype(jnp.int32)

        @pl.when(near)
        def _():
            pl.semaphore_signal(barrier, inc=1, device_id=(me, row + row_step), device_id_type=MESH)

        @pl.when(far)
        def _():
            for step in range(N_TM):
                pl.semaphore_signal(
                    barrier, inc=1, device_id=(lax.rem(me + step, N_TM), row + row_step), device_id_type=MESH
                )

    lane = lax.broadcasted_iota(jnp.int32, (1, 128), 1)
    held = jnp.zeros((1, 128), jnp.int32)
    for slot in range(F):
        held = jnp.where(lane == slot, slots[slot], held)
    labels[0:1] = held

    loads[0].wait()
    gain = gain_one[...]
    gain_low = gain[:, :128]
    gain_pairs = jnp.concatenate([gain[:, 128:], gain[:, 128:]], axis=1)
    for slot in range(F):
        for line in range(2):
            span_of = slice(line * PACK, (line + 1) * PACK)
            block = gathered(frames[slot, line])
            packed[slot, span_of] = block
            packed_first[slot, span_of] = norm_packed(block, gain_low, gain_pairs)
    for step in range(N_TM):
        target = lax.rem(me + step, N_TM)
        count = jnp.int32(0)
        picks = [jnp.int32(0), jnp.int32(0)]
        for slot in range(F):
            mine = lax.shift_right_logical(slots[slot], 3) == target
            for rank in range(2):
                picks[rank] = jnp.where(jnp.logical_and(mine, count == rank), slot, picks[rank])
            count = count + mine.astype(jnp.int32)
        for rank in range(2):
            at = 2 * step + rank
            outgoing_first[at] = packed_first[picks[rank]]
            if step:
                outgoing[at] = packed[picks[rank]]
            else:
                arrived[rank] = packed[picks[rank]]
                first[rank] = packed_first[picks[rank]]

    pl.semaphore_wait(barrier, peers)

    def pair_of(ref, step):
        return ref.at[pl.ds(2 * step, 2)]

    label_copies, frame_copies, up_near, up_far, down_near, down_far = {}, {}, {}, {}, {}, {}
    for step in range(N_TM):
        target = lax.rem(me + step, N_TM)
        if step:
            label_copies[step] = remote(
                labels.at[pl.ds(0, 1)], labels.at[pl.ds(step, 1)], l_send.at[step], l_recv.at[step], target, row
            )
            frame_copies[step] = remote(
                pair_of(outgoing, step), pair_of(arrived, step), a_send.at[step], a_recv.at[step], target, row
            )
        up_near[step] = remote(
            pair_of(first, step), pair_of(down_first, step), up_send.at[step], up_recv.at[step], me, row - 1
        )
        down_near[step] = remote(
            pair_of(first, step), pair_of(up_first, step), down_send.at[step], down_recv.at[step], me, row + 1
        )
        up_far[step] = remote(
            pair_of(outgoing_first, step), pair_of(down_first, step), up_send.at[step], up_recv.at[step],
            target, row - 1,
        )
        down_far[step] = remote(
            pair_of(outgoing_first, step), pair_of(up_first, step), down_send.at[step], down_recv.at[step],
            target, row + 1,
        )

    def forward(step):
        @pl.when(near_up)
        def _():
            up_near[step].start()

        @pl.when(near_down)
        def _():
            down_near[step].start()

    for step in ORDER:
        label_copies[step].start()
    for step in ORDER:
        frame_copies[step].start()
    for far, copies in ((far_up, up_far), (far_down, down_far)):

        @pl.when(far)
        def _():
            for step in ORDER + (0,):
                copies[step].start()

    forward(0)

    @pl.when(jnp.logical_not(has_up))
    def _():
        up_first[...] = jnp.zeros_like(up_first)

    @pl.when(jnp.logical_not(has_down))
    def _():
        down_first[...] = jnp.zeros_like(down_first)

    @pl.when(jnp.logical_not(has_before))
    def _():
        tail_before[...] = jnp.zeros_like(tail_before)
        second_before[...] = jnp.zeros_like(second_before)

    for step in ORDER:
        label_copies[step].wait_recv()
    to_scalars = pltpu.make_async_copy(labels, labels_s, label_sem)
    to_scalars.start()
    to_scalars.wait()

    def scan_source(step, places):
        count = jnp.int32(0)
        for slot in range(F):
            held = labels_s[step, slot]
            mine = lax.shift_right_logical(held, 3) == me
            local = jnp.bitwise_and(held, F - 1)
            at = 2 * step + jnp.minimum(count, 1)
            places = tuple(jnp.where(jnp.logical_and(mine, local == f), at, places[f]) for f in range(F))
            count = count + mine.astype(jnp.int32)
        return places

    places = lax.fori_loop(0, N_TM, scan_source, (jnp.int32(0),) * F)

    opened = []
    for span in range(2):
        start, hit = jnp.int32(0), jnp.bool_(False)
        for shot in range(4):
            hit = jnp.logical_or(hit, start == 2 * me + span)
            start = start + spans[shot]
        opened.append(hit)

    for step in ORDER:
        frame_copies[step].wait_recv()
        for rank in range(2):
            for line in range(2):
                span_of = slice(line * PACK, (line + 1) * PACK)
                first[2 * step + rank, span_of] = norm_packed(
                    arrived[2 * step + rank, span_of], gain_low, gain_pairs
                )
        forward(step)

    def tail_copy(side):
        return remote(tail.at[side], tail_before.at[side], t_send.at[side], t_recv.at[side], me + 1, row)

    for k in range(2):
        tail[0, k] = first[places[F - 2 + k]]

    @pl.when(has_next)
    def _():
        tail_copy(0).start()

    for has_side, copies in ((has_down, up_near), (has_up, down_near)):

        @pl.when(has_side)
        def _():
            for step in (0,) + ORDER:
                copies[step].wait_recv()

    for k in range(2):
        tail[1, k] = up_first[places[F - 2 + k]]
        tail[2, k] = down_first[places[F - 2 + k]]

    @pl.when(has_next)
    def _():
        tail_copy(1).start()
        tail_copy(2).start()

    def place(f):
        for source, base in ((first, 2), (up_first, 0), (down_first, 4)):
            block = source[places[f]]
            for line in range(2):
                value = spread(block[line * PACK : (line + 1) * PACK])
                grid_one[(2 if f < SPAN else 4) + f, base + line] = value
                if f in (2, 3):
                    grid_one[4 + f, base + line] = jnp.where(opened[1], jnp.zeros_like(value), value)

    line_of = lax.broadcasted_iota(jnp.int32, (2 * 4 * COLS, 1), 0) // COLS % 4
    outside = jnp.logical_or(
        jnp.logical_and(line_of == 0, jnp.logical_not(has_up)),
        jnp.logical_and(line_of == 3, jnp.logical_not(has_down)),
    )

    def second_of(base):
        hidden = conv(grid_one, base, 2, 4, w_one) + bias_one[...]
        mean = jnp.sum(hidden * hidden, axis=-1, keepdims=True) * (1.0 / CH)
        second = silu(hidden * lax.rsqrt(mean + 1e-06) * gain_two[...])
        second = jnp.where(outside, 0.0, second).astype(BF16).reshape(2, 4, COLS, CH)
        grid_two[base + 2 : base + 4] = second
        return second

    def finish(span):
        branch = conv(grid_two, 6 * span, SPAN, 2, w_two) + bias_two[...]
        for f in range(SPAN):
            block = arrived[places[SPAN * span + f]]
            for line in range(2):
                held = spread(block[line * PACK : (line + 1) * PACK]).astype(F32)
                at = (2 * f + line) * COLS
                out[SPAN * span + f, line] = (held + branch[at : at + COLS]).astype(BF16)

    for f in (4, 5, 6, 7):
        place(f)
    loads[1].wait()
    second = second_of(8)
    for k in range(2):
        for line in range(4):
            second_tail[k, line * PACK : (line + 1) * PACK] = gathered(second[k, line])
    send_second = remote(second_tail, second_before, s_send, s_recv, me + 1, row)

    @pl.when(has_next)
    def _():
        send_second.start()

    for f in (2, 3):
        place(f)
    second_of(6)
    for f in (0, 1):
        place(f)
    second = second_of(2)
    grid_two[6:8] = jnp.where(opened[1], jnp.zeros_like(second), second)
    loads[2].wait()
    finish(1)

    @pl.when(has_before)
    def _():
        for side in range(3):
            tail_copy(side).wait_recv()

    for side, base in ((0, 2), (1, 0), (2, 4)):
        for k in range(2):
            for line in range(2):
                value = spread(tail_before[side, k, line * PACK : (line + 1) * PACK])
                grid_one[k, base + line] = jnp.where(opened[0], jnp.zeros_like(value), value)
    second_of(0)

    @pl.when(has_before)
    def _():
        send_second.wait_recv()

    for k in range(2):
        for line in range(4):
            value = spread(second_before[k, line * PACK : (line + 1) * PACK])
            grid_two[k, line] = jnp.where(opened[0], jnp.zeros_like(value), value)
    finish(0)

    for step in ORDER:
        label_copies[step].wait_send()
        frame_copies[step].wait_send()
    for has_side, copies in ((has_up, up_near), (has_down, down_near)):

        @pl.when(has_side)
        def _():
            for step in (0,) + ORDER:
                copies[step].wait_send()

    @pl.when(has_next)
    def _():
        for side in range(3):
            tail_copy(side).wait_send()
        send_second.wait_send()


def body(
    frames_in, slot_frame, shot_spans, gain_one, conv_one, bias_one, gain_two, conv_two, bias_two
):
    vmem, smem, dma = pltpu.VMEM, pltpu.SMEM, pltpu.SemaphoreType.DMA
    whole = pl.BlockSpec(memory_space=vmem)
    hbm, scalars = pl.BlockSpec(memory_space=pl.ANY), pl.BlockSpec(memory_space=smem)
    taps, vector = (27, CH, CH), (1, CH)
    blocks = vmem((2 * N_TM, 2 * PACK, 128), BF16)
    return pl.pallas_call(
        functools.partial(kernel, lax.axis_size("rows")),
        out_shape=jax.ShapeDtypeStruct(frames_in.shape, BF16),
        in_specs=[hbm, scalars, scalars, whole, hbm, whole, whole, hbm, whole],
        out_specs=whole,
        scratch_shapes=[
            vmem(frames_in.shape, BF16),
            vmem(taps, BF16),
            vmem(taps, BF16),
            vmem((F, 2 * PACK, 128), BF16),
            vmem((F, 2 * PACK, 128), BF16),
            blocks, blocks, blocks, blocks, blocks, blocks,
            vmem((N_TM, 128), jnp.int32),
            smem((N_TM, 128), jnp.int32),
            vmem((3, 2, 2 * PACK, 128), BF16),
            vmem((3, 2, 2 * PACK, 128), BF16),
            vmem((2, 4 * PACK, 128), BF16),
            vmem((2, 4 * PACK, 128), BF16),
            vmem((12, 6, COLS, CH), BF16),
            vmem((12, 4, COLS, CH), BF16),
            dma((3,)),
            dma,
            dma((N_TM,)), dma((N_TM,)),
            dma((N_TM,)), dma((N_TM,)),
            dma((N_TM,)), dma((N_TM,)),
            dma((N_TM,)), dma((N_TM,)),
            dma((3,)), dma((3,)),
            dma, dma,
        ],
        name="residual_block",
        compiler_params=pltpu.CompilerParams(
            collective_id=1, has_side_effects=True, vmem_limit_bytes=60 << 20
        ),
    )(
        frames_in, slot_frame, shot_spans, gain_one.reshape(vector),
        conv_one.reshape(taps), bias_one.reshape(vector), gain_two.reshape(vector),
        conv_two.reshape(taps), bias_two.reshape(vector),
    )


def solution(mesh):
    placed = (P("tm", "rows", None, None), P("tm"), P(), P(), P(), P(), P(), P(), P())
    return jax.shard_map(
        body, mesh=mesh, in_specs=placed, out_specs=P("tm", "rows", None, None), check_vma=False
    )
```

```python
import functools

import jax
import jax.numpy as jnp
from jax import lax
from jax.experimental import pallas as pl
from jax.experimental.pallas import tpu as pltpu
from jax.sharding import PartitionSpec as P

SPAN = 4
CH = 192
COLS = 32
N_TM = 8
F = 8
PACK = 48
ORDER = (1, 7, 2, 6, 3, 5, 4)
WINDOW = 4
F32 = jnp.float32
BF16 = jnp.bfloat16
MESH = pl.DeviceIdType.MESH


def remote(src, dst, send, recv, tm, rows):
    return pltpu.make_async_remote_copy(
        src_ref=src, dst_ref=dst, send_sem=send, recv_sem=recv, device_id=(tm, rows), device_id_type=MESH
    )


def silu(u):
    return u / (1.0 + jnp.exp(-u))


def spread(packed):
    low, pairs = packed[:COLS], packed[COLS:]
    high = jnp.concatenate([pairs[:, :64], pairs[:, 64:]], axis=0)
    return jnp.concatenate([low, high], axis=1)


def gathered(image_row):
    high = image_row[:, 128:]
    pairs = jnp.concatenate([high[:16], high[16:]], axis=1)
    return jnp.concatenate([image_row[:, :128], pairs], axis=0)


def norm_packed(packed, gain_low, gain_pairs):
    values = packed.astype(F32)
    low, pairs = values[:COLS], values[COLS:]
    left = lax.broadcasted_iota(jnp.int32, pairs.shape, 1) < 64
    low_sum = jnp.sum(low * low, axis=-1, keepdims=True)
    squares = pairs * pairs
    left_sum = jnp.sum(jnp.where(left, squares, 0.0), axis=-1, keepdims=True)
    right_sum = jnp.sum(jnp.where(left, 0.0, squares), axis=-1, keepdims=True)
    total = low_sum + jnp.concatenate([left_sum, right_sum], axis=0)
    scale = lax.rsqrt(total * (1.0 / CH) + 1e-06)
    low_out = silu(low * scale * gain_low)
    pairs_out = silu(pairs * jnp.where(left, scale[:16], scale[16:]) * gain_pairs)
    return jnp.concatenate([low_out.astype(BF16), pairs_out.astype(BF16)], axis=0)


def col_taps(left, middle, right):
    count = middle.shape[0]
    col = lax.broadcasted_iota(jnp.int32, middle.shape, 0) % COLS
    from_left = jnp.where(col == 0, 0.0, pltpu.roll(left, 1, 0))
    from_right = jnp.where(col == COLS - 1, 0.0, pltpu.roll(right, count - 1, 0))
    return middle + from_left + from_right


def conv(source, base, frames, rows, weight, time_taps):
    count = frames * rows * COLS
    sums = [jnp.zeros((count, CH), F32) for _ in range(3)]
    for time_tap in time_taps:
        at = base if len(time_taps) == 1 else base + time_tap
        for row_tap in range(3):
            tile = source[pl.ds(at, frames), pl.ds(row_tap, rows)].reshape(count, CH)
            for col_tap in range(3):
                tap = weight[(time_tap * 3 + row_tap) * 3 + col_tap]
                sums[col_tap] = sums[col_tap] + jnp.dot(tile, tap, preferred_element_type=F32)
    return col_taps(*sums)


def kernel(
    n_rows,
    frames_h, slots, spans, gain_one_h, conv_one_h, bias_one_h, gain_two_h, conv_two_h, bias_two_h,
    out,
    frames, gain_one, w_one, bias_one, gain_two, w_two, bias_two,
    packed, packed_first, outgoing, outgoing_first, arrived, first, up_first, down_first,
    labels, labels_s, tail, tail_before, second_tail, second_before, grid_one, grid_tail, parts, grid_two,
    in_sem, label_sem, l_send, l_recv, a_send, a_recv, up_send, up_recv, down_send, down_recv,
    t_send, t_recv, s_send, s_recv, gate_sem, line_sem,
):
    me = lax.axis_index("tm")
    row = lax.axis_index("rows")
    has_up, has_down = row > 0, row < n_rows - 1
    has_next, has_before = me < N_TM - 1, me > 0
    far_up, far_down = row == n_rows // 2, row == n_rows // 2 - 1
    far = jnp.logical_or(far_up, far_down)
    ends = jnp.logical_or(me == 0, me == N_TM - 1)
    near_up = jnp.logical_and(has_up, jnp.logical_not(far_up))
    near_down = jnp.logical_and(has_down, jnp.logical_not(far_down))

    barrier = pltpu.get_barrier_semaphore()
    peers = jnp.int32(N_TM - 1)
    for near, across, row_step in ((near_up, far_up, -1), (near_down, far_down, 1)):
        greets = jnp.logical_and(across, ends)
        peers = peers + near.astype(jnp.int32) + greets.astype(jnp.int32)

        @pl.when(near)
        def _():
            pl.semaphore_signal(barrier, inc=1, device_id=(me, row + row_step), device_id_type=MESH)

        @pl.when(greets)
        def _():
            pl.semaphore_signal(
                barrier, inc=1, device_id=(N_TM - 1 - me, row + row_step), device_id_type=MESH
            )

    for step in ORDER:
        pl.semaphore_signal(barrier, inc=1, device_id=(lax.rem(me + step, N_TM), row), device_id_type=MESH)

    loads = [
        pltpu.make_async_copy(src, dst, in_sem.at[i])
        for i, (src, dst) in enumerate((
            (frames_h, frames), (gain_one_h, gain_one), (bias_one_h, bias_one), (gain_two_h, gain_two),
            (bias_two_h, bias_two), (conv_one_h, w_one), (conv_two_h, w_two),
        ))
    ]
    for load in loads:
        load.start()

    lane = lax.broadcasted_iota(jnp.int32, (1, 128), 1)
    held = jnp.zeros((1, 128), jnp.int32)
    for slot in range(F):
        held = jnp.where(lane == slot, slots[slot], held)
    labels[0:1] = held

    loads[0].wait()
    loads[1].wait()
    gain = gain_one[...]
    gain_low = gain[:, :128]
    gain_pairs = jnp.concatenate([gain[:, 128:], gain[:, 128:]], axis=1)
    for slot in range(F):
        for line in range(2):
            span_of = slice(line * PACK, (line + 1) * PACK)
            block = gathered(frames[slot, line])
            packed[slot, span_of] = block
            packed_first[slot, span_of] = norm_packed(block, gain_low, gain_pairs)
    for step in range(N_TM):
        target = lax.rem(me + step, N_TM)
        count = jnp.int32(0)
        picks = [jnp.int32(0), jnp.int32(0)]
        for slot in range(F):
            mine = lax.shift_right_logical(slots[slot], 3) == target
            for rank in range(2):
                picks[rank] = jnp.where(jnp.logical_and(mine, count == rank), slot, picks[rank])
            count = count + mine.astype(jnp.int32)
        for rank in range(2):
            at = 2 * step + rank
            outgoing_first[at] = packed_first[picks[rank]]
            if step:
                outgoing[at] = packed[picks[rank]]
            else:
                arrived[rank] = packed[picks[rank]]
                first[rank] = packed_first[picks[rank]]

    pl.semaphore_wait(barrier, peers)

    def pair_of(ref, step):
        return ref.at[pl.ds(2 * step, 2)]

    label_copies, frame_copies, up_near, up_far, down_near, down_far = {}, {}, {}, {}, {}, {}
    for step in range(N_TM):
        target = lax.rem(me + step, N_TM)
        if step:
            label_copies[step] = remote(
                labels.at[pl.ds(0, 1)], labels.at[pl.ds(step, 1)], l_send.at[step], l_recv.at[step], target, row
            )
            frame_copies[step] = remote(
                pair_of(outgoing, step), pair_of(arrived, step), a_send.at[step], a_recv.at[step], target, row
            )
        up_near[step] = remote(
            pair_of(first, step), pair_of(down_first, step), up_send.at[step], up_recv.at[step], me, row - 1
        )
        down_near[step] = remote(
            pair_of(first, step), pair_of(up_first, step), down_send.at[step], down_recv.at[step], me, row + 1
        )
        up_far[step] = remote(
            pair_of(outgoing_first, step), pair_of(down_first, step), up_send.at[step], up_recv.at[step],
            target, row - 1,
        )
        down_far[step] = remote(
            pair_of(outgoing_first, step), pair_of(up_first, step), down_send.at[step], down_recv.at[step],
            target, row + 1,
        )

    def forward(step):
        @pl.when(near_up)
        def _():
            up_near[step].start()

        @pl.when(near_down)
        def _():
            down_near[step].start()

    for step in ORDER:
        label_copies[step].start()
    order = (0,) + ORDER
    for step in order[1 : WINDOW + 1]:
        frame_copies[step].start()

    for across, row_step in ((far_up, -1), (far_down, 1)):

        @pl.when(jnp.logical_and(across, ends))
        def _():
            pl.semaphore_signal(
                gate_sem, inc=1, device_id=(N_TM - 1 - me, row + row_step), device_id_type=MESH
            )

    @pl.when(jnp.logical_and(far, ends))
    def _():
        pl.semaphore_wait(gate_sem, 1)
        for distance in range(1, N_TM // 2):
            target = jnp.where(me == 0, me + distance, me - distance)
            pl.semaphore_signal(line_sem, inc=1, device_id=(target, row), device_id_type=MESH)

    forward(0)

    @pl.when(jnp.logical_not(has_up))
    def _():
        up_first[...] = jnp.zeros_like(up_first)

    @pl.when(jnp.logical_not(has_down))
    def _():
        down_first[...] = jnp.zeros_like(down_first)

    @pl.when(jnp.logical_not(has_before))
    def _():
        tail_before[...] = jnp.zeros_like(tail_before)
        second_before[...] = jnp.zeros_like(second_before)

    opened = []
    for span in range(2):
        start, hit = jnp.int32(0), jnp.bool_(False)
        for shot in range(4):
            hit = jnp.logical_or(hit, start == 2 * me + span)
            start = start + spans[shot]
        opened.append(hit)

    def find_places():
        for step in ORDER:
            label_copies[step].wait_recv()
        to_scalars = pltpu.make_async_copy(labels, labels_s, label_sem)
        to_scalars.start()
        to_scalars.wait()

        def scan_source(step, places):
            count = jnp.int32(0)
            for slot in range(F):
                held = labels_s[step, slot]
                mine = lax.shift_right_logical(held, 3) == me
                local = jnp.bitwise_and(held, F - 1)
                at = 2 * step + jnp.minimum(count, 1)
                places = tuple(jnp.where(jnp.logical_and(mine, local == f), at, places[f]) for f in range(F))
                count = count + mine.astype(jnp.int32)
            return places

        return lax.fori_loop(0, N_TM, scan_source, (jnp.int32(0),) * F)

    def take_in(step):
        frame_copies[step].wait_recv()
        for rank in range(2):
            for line in range(2):
                span_of = slice(line * PACK, (line + 1) * PACK)
                first[2 * step + rank, span_of] = norm_packed(
                    arrived[2 * step + rank, span_of], gain_low, gain_pairs
                )
        forward(step)

    def wait_halo(step):
        for has_side, copies in ((has_down, up_near), (has_up, down_near)):

            @pl.when(has_side)
            def _():
                copies[step].wait_recv()

    def convolve_pair(at, slots_of):
        for k in range(2):
            for source, base in ((first, 2), (up_first, 0), (down_first, 4)):
                block = source[slots_of[k]]
                for line in range(2):
                    grid_one[at + k, base + line] = spread(block[line * PACK : (line + 1) * PACK])
        for time_tap in range(3):
            share = conv(grid_one, at, 2, 4, w_one, (time_tap,))
            parts[time_tap, at : at + 2] = share.reshape(2, 4, COLS, CH)

    def convolve(step):
        convolve_pair(2 * step, (2 * step, 2 * step + 1))

    def convolve_video(f):
        convolve_pair(f, places[f : f + 2])

    for i in range(1, N_TM):
        take_in(order[i])
        if i + WINDOW < N_TM:
            frame_copies[order[i]].wait_send()
            frame_copies[order[i + WINDOW]].start()
        if i == 1:

            @pl.when(jnp.logical_and(far, jnp.logical_not(ends)))
            def _():
                pl.semaphore_wait(line_sem, 1)

            for across, copies in ((far_up, up_far), (far_down, down_far)):

                @pl.when(across)
                def _():
                    for step in order:
                        copies[step].start()

        if i == 2:
            loads[5].wait()
            places = find_places()
        if i >= 2:

            @pl.when(jnp.logical_not(far))
            def _():
                wait_halo(order[i - 2])
                convolve(order[i - 2])

    def tail_copy(side):
        return remote(tail.at[side], tail_before.at[side], t_send.at[side], t_recv.at[side], me + 1, row)

    for k in range(2):
        tail[0, k] = first[places[F - 2 + k]]

    @pl.when(has_next)
    def _():
        tail_copy(0).start()

    @pl.when(jnp.logical_not(far))
    def _():
        wait_halo(order[-2])
        convolve(order[-2])
        wait_halo(order[-1])

    @pl.when(far)
    def _():
        for step in order:
            wait_halo(step)

    for k in range(2):
        tail[1, k] = up_first[places[F - 2 + k]]
        tail[2, k] = down_first[places[F - 2 + k]]

    @pl.when(has_next)
    def _():
        tail_copy(1).start()
        tail_copy(2).start()

    @pl.when(jnp.logical_not(far))
    def _():
        convolve(order[-1])

    @pl.when(far)
    def _():
        convolve_video(6)
        convolve_video(4)

    spots = [jnp.where(far, f, places[f]) for f in range(F)]
    for load in loads[2:5]:
        load.wait()

    line_of = lax.broadcasted_iota(jnp.int32, (2 * 4 * COLS, 1), 0) // COLS % 4
    outside = jnp.logical_or(
        jnp.logical_and(line_of == 0, jnp.logical_not(has_up)),
        jnp.logical_and(line_of == 3, jnp.logical_not(has_down)),
    )

    def part(time_tap, f):
        return parts[time_tap, spots[f]].reshape(4 * COLS, CH)

    def cut(span, share):
        return jnp.where(opened[span], jnp.zeros_like(share), share)

    def second_of(at, hidden):
        hidden = jnp.concatenate(hidden, axis=0) + bias_one[...]
        mean = jnp.sum(hidden * hidden, axis=-1, keepdims=True) * (1.0 / CH)
        second = silu(hidden * lax.rsqrt(mean + 1e-06) * gain_two[...])
        second = jnp.where(outside, 0.0, second).astype(BF16).reshape(2, 4, COLS, CH)
        grid_two[at : at + 2] = second
        return second

    def whole(f):
        return part(2, f) + part(1, f - 1) + part(0, f - 2)

    def finish(span):
        branch = conv(grid_two, 6 * span, SPAN, 2, w_two, (0, 1, 2)) + bias_two[...]
        for f in range(SPAN):
            block = arrived[places[SPAN * span + f]]
            for line in range(2):
                held = spread(block[line * PACK : (line + 1) * PACK]).astype(F32)
                at = (2 * f + line) * COLS
                out[SPAN * span + f, line] = (held + branch[at : at + COLS]).astype(BF16)

    second = second_of(10, [whole(6), whole(7)])
    for k in range(2):
        for line in range(4):
            second_tail[k, line * PACK : (line + 1) * PACK] = gathered(second[k, line])
    send_second = remote(second_tail, second_before, s_send, s_recv, me + 1, row)

    @pl.when(has_next)
    def _():
        send_second.start()

    @pl.when(far)
    def _():
        convolve_video(2)
        convolve_video(0)

    second_of(8, [
        part(2, 4) + cut(1, part(1, 3) + part(0, 2)),
        part(2, 5) + part(1, 4) + cut(1, part(0, 3)),
    ])
    second = second_of(4, [whole(2), whole(3)])
    grid_two[6:8] = jnp.where(opened[1], jnp.zeros_like(second), second)
    loads[6].wait()
    finish(1)

    @pl.when(has_before)
    def _():
        for side in range(3):
            tail_copy(side).wait_recv()

    for side, base in ((0, 2), (1, 0), (2, 4)):
        for k in range(2):
            for line in range(2):
                grid_tail[k, base + line] = spread(tail_before[side, k, line * PACK : (line + 1) * PACK])
    two_back = conv(grid_tail, 0, 2, 4, w_one, (0,))
    one_back = conv(grid_tail, 1, 1, 4, w_one, (1,))
    second_of(2, [
        part(2, 0) + cut(0, one_back + two_back[: 4 * COLS]),
        part(2, 1) + part(1, 0) + cut(0, two_back[4 * COLS :]),
    ])

    @pl.when(has_before)
    def _():
        send_second.wait_recv()

    for k in range(2):
        for line in range(4):
            value = spread(second_before[k, line * PACK : (line + 1) * PACK])
            grid_two[k, line] = jnp.where(opened[0], jnp.zeros_like(value), value)
    finish(0)

    for step in ORDER:
        label_copies[step].wait_send()
    for step in order[N_TM - WINDOW :]:
        frame_copies[step].wait_send()
    for has_side, copies in ((has_up, up_near), (has_down, down_near)):

        @pl.when(has_side)
        def _():
            for step in order:
                copies[step].wait_send()

    @pl.when(has_next)
    def _():
        for side in range(3):
            tail_copy(side).wait_send()
        send_second.wait_send()


def body(
    frames_in, slot_frame, shot_spans, gain_one, conv_one, bias_one, gain_two, conv_two, bias_two
):
    vmem, smem, dma = pltpu.VMEM, pltpu.SMEM, pltpu.SemaphoreType.DMA
    whole = pl.BlockSpec(memory_space=vmem)
    hbm, scalars = pl.BlockSpec(memory_space=pltpu.HBM), pl.BlockSpec(memory_space=smem)
    taps, vector = (27, CH, CH), (1, CH)
    blocks = vmem((2 * N_TM, 2 * PACK, 128), BF16)
    return pl.pallas_call(
        functools.partial(kernel, lax.axis_size("rows")),
        out_shape=jax.ShapeDtypeStruct(frames_in.shape, BF16),
        in_specs=[hbm, scalars, scalars] + [hbm] * 6,
        out_specs=whole,
        scratch_shapes=[
            vmem(frames_in.shape, BF16),
            vmem(vector, F32),
            vmem(taps, BF16),
            vmem(vector, F32),
            vmem(vector, F32),
            vmem(taps, BF16),
            vmem(vector, F32),
            vmem((F, 2 * PACK, 128), BF16),
            vmem((F, 2 * PACK, 128), BF16),
            blocks, blocks, blocks, blocks, blocks, blocks,
            vmem((N_TM, 128), jnp.int32),
            smem((N_TM, 128), jnp.int32),
            vmem((3, 2, 2 * PACK, 128), BF16),
            vmem((3, 2, 2 * PACK, 128), BF16),
            vmem((2, 4 * PACK, 128), BF16),
            vmem((2, 4 * PACK, 128), BF16),
            vmem((2 * N_TM, 6, COLS, CH), BF16),
            vmem((2, 6, COLS, CH), BF16),
            vmem((3, 2 * N_TM, 4, COLS, CH), F32),
            vmem((12, 4, COLS, CH), BF16),
            dma((7,)),
            dma,
            dma((N_TM,)), dma((N_TM,)),
            dma((N_TM,)), dma((N_TM,)),
            dma((N_TM,)), dma((N_TM,)),
            dma((N_TM,)), dma((N_TM,)),
            dma((3,)), dma((3,)),
            dma, dma,
            pltpu.SemaphoreType.REGULAR, pltpu.SemaphoreType.REGULAR,
        ],
        name="residual_block",
        compiler_params=pltpu.CompilerParams(
            collective_id=1, has_side_effects=True, vmem_limit_bytes=60 << 20
        ),
    )(
        frames_in, slot_frame, shot_spans, gain_one.reshape(vector),
        conv_one.reshape(taps), bias_one.reshape(vector), gain_two.reshape(vector),
        conv_two.reshape(taps), bias_two.reshape(vector),
    )


def solution(mesh):
    placed = (P("tm", "rows", None, None), P("tm"), P(), P(), P(), P(), P(), P(), P())
    return jax.shard_map(
        body, mesh=mesh, in_specs=placed, out_specs=P("tm", "rows", None, None), check_vma=False
    )
```

```python
import functools

import jax
import jax.numpy as jnp
from jax import lax
from jax.experimental import pallas as pl
from jax.experimental.pallas import tpu as pltpu
from jax.sharding import PartitionSpec as P

SPAN = 4
CH = 192
COLS = 32
N_TM = 8
F = 8
PACK = 48
ORDER = (1, 7, 2, 6, 3, 5, 4)
WINDOW = 4
F32 = jnp.float32
BF16 = jnp.bfloat16
MESH = pl.DeviceIdType.MESH


def remote(src, dst, send, recv, tm, rows):
    return pltpu.make_async_remote_copy(
        src_ref=src, dst_ref=dst, send_sem=send, recv_sem=recv, device_id=(tm, rows), device_id_type=MESH
    )


def silu(u):
    return u / (1.0 + jnp.exp(-u))


def spread(packed):
    low, pairs = packed[:COLS], packed[COLS:]
    high = jnp.concatenate([pairs[:, :64], pairs[:, 64:]], axis=0)
    return jnp.concatenate([low, high], axis=1)


def gathered(image_row):
    high = image_row[:, 128:]
    pairs = jnp.concatenate([high[:16], high[16:]], axis=1)
    return jnp.concatenate([image_row[:, :128], pairs], axis=0)


def norm_packed(packed, gain_low, gain_pairs):
    values = packed.astype(F32)
    low, pairs = values[:COLS], values[COLS:]
    left = lax.broadcasted_iota(jnp.int32, pairs.shape, 1) < 64
    low_sum = jnp.sum(low * low, axis=-1, keepdims=True)
    squares = pairs * pairs
    left_sum = jnp.sum(jnp.where(left, squares, 0.0), axis=-1, keepdims=True)
    right_sum = jnp.sum(jnp.where(left, 0.0, squares), axis=-1, keepdims=True)
    total = low_sum + jnp.concatenate([left_sum, right_sum], axis=0)
    scale = lax.rsqrt(total * (1.0 / CH) + 1e-06)
    low_out = silu(low * scale * gain_low)
    pairs_out = silu(pairs * jnp.where(left, scale[:16], scale[16:]) * gain_pairs)
    return jnp.concatenate([low_out.astype(BF16), pairs_out.astype(BF16)], axis=0)


def col_taps(left, middle, right):
    count = middle.shape[0]
    col = lax.broadcasted_iota(jnp.int32, middle.shape, 0) % COLS
    from_left = jnp.where(col == 0, 0.0, pltpu.roll(left, 1, 0))
    from_right = jnp.where(col == COLS - 1, 0.0, pltpu.roll(right, count - 1, 0))
    return middle + from_left + from_right


def conv(source, base, frames, rows, weight, time_taps, first_row=0):
    count = frames * rows * COLS
    sums = [jnp.zeros((count, CH), F32) for _ in range(3)]
    for time_tap in time_taps:
        at = base if len(time_taps) == 1 else base + time_tap
        for row_tap in range(3):
            tile = source[pl.ds(at, frames), pl.ds(first_row + row_tap, rows)].reshape(count, CH)
            for col_tap in range(3):
                tap = weight[(time_tap * 3 + row_tap) * 3 + col_tap]
                sums[col_tap] = sums[col_tap] + jnp.dot(tile, tap, preferred_element_type=F32)
    return col_taps(*sums)


def kernel(
    n_rows,
    frames_h, slots, spans, gain_one_h, conv_one_h, bias_one_h, gain_two_h, conv_two_h, bias_two_h,
    out,
    frames, gain_one, w_one, bias_one, gain_two, w_two, bias_two,
    packed, packed_first, outgoing, outgoing_first, arrived, first, up_first, down_first,
    labels, labels_s, tail, tail_before, second_tail, second_before, grid_one, grid_tail, parts, grid_two,
    in_sem, label_sem, l_send, l_recv, a_send, a_recv, up_send, up_recv, down_send, down_recv,
    t_send, t_recv, s_send, s_recv, gate_sem, line_sem,
):
    me = lax.axis_index("tm")
    row = lax.axis_index("rows")
    has_up, has_down = row > 0, row < n_rows - 1
    has_next, has_before = me < N_TM - 1, me > 0
    far_up, far_down = row == n_rows // 2, row == n_rows // 2 - 1
    far = jnp.logical_or(far_up, far_down)
    ends = jnp.logical_or(me == 0, me == N_TM - 1)
    near_up = jnp.logical_and(has_up, jnp.logical_not(far_up))
    near_down = jnp.logical_and(has_down, jnp.logical_not(far_down))

    barrier = pltpu.get_barrier_semaphore()
    peers = jnp.int32(N_TM - 1)
    for near, across, row_step in ((near_up, far_up, -1), (near_down, far_down, 1)):
        greets = jnp.logical_and(across, ends)
        peers = peers + near.astype(jnp.int32) + greets.astype(jnp.int32)

        @pl.when(near)
        def _():
            pl.semaphore_signal(barrier, inc=1, device_id=(me, row + row_step), device_id_type=MESH)

        @pl.when(greets)
        def _():
            pl.semaphore_signal(
                barrier, inc=1, device_id=(N_TM - 1 - me, row + row_step), device_id_type=MESH
            )

    for step in ORDER:
        pl.semaphore_signal(barrier, inc=1, device_id=(lax.rem(me + step, N_TM), row), device_id_type=MESH)

    loads = [
        pltpu.make_async_copy(src, dst, in_sem.at[i])
        for i, (src, dst) in enumerate((
            (frames_h, frames), (gain_one_h, gain_one), (bias_one_h, bias_one), (gain_two_h, gain_two),
            (bias_two_h, bias_two), (conv_one_h, w_one), (conv_two_h, w_two),
        ))
    ]
    for load in loads:
        load.start()

    lane = lax.broadcasted_iota(jnp.int32, (1, 128), 1)
    held = jnp.zeros((1, 128), jnp.int32)
    for slot in range(F):
        held = jnp.where(lane == slot, slots[slot], held)
    labels[0:1] = held

    loads[0].wait()
    loads[1].wait()
    gain = gain_one[...]
    gain_low = gain[:, :128]
    gain_pairs = jnp.concatenate([gain[:, 128:], gain[:, 128:]], axis=1)
    for slot in range(F):
        for line in range(2):
            span_of = slice(line * PACK, (line + 1) * PACK)
            block = gathered(frames[slot, line])
            packed[slot, span_of] = block
            packed_first[slot, span_of] = norm_packed(block, gain_low, gain_pairs)
    for step in range(N_TM):
        target = lax.rem(me + step, N_TM)
        count = jnp.int32(0)
        picks = [jnp.int32(0), jnp.int32(0)]
        for slot in range(F):
            mine = lax.shift_right_logical(slots[slot], 3) == target
            for rank in range(2):
                picks[rank] = jnp.where(jnp.logical_and(mine, count == rank), slot, picks[rank])
            count = count + mine.astype(jnp.int32)
        for rank in range(2):
            at = 2 * step + rank
            outgoing_first[at] = packed_first[picks[rank]]
            if step:
                outgoing[at] = packed[picks[rank]]
            else:
                arrived[rank] = packed[picks[rank]]
                first[rank] = packed_first[picks[rank]]

    pl.semaphore_wait(barrier, peers)

    def pair_of(ref, step):
        return ref.at[pl.ds(2 * step, 2)]

    label_copies, frame_copies, up_near, up_far, down_near, down_far = {}, {}, {}, {}, {}, {}
    for step in range(N_TM):
        target = lax.rem(me + step, N_TM)
        if step:
            label_copies[step] = remote(
                labels.at[pl.ds(0, 1)], labels.at[pl.ds(step, 1)], l_send.at[step], l_recv.at[step], target, row
            )
            frame_copies[step] = remote(
                pair_of(outgoing, step), pair_of(arrived, step), a_send.at[step], a_recv.at[step], target, row
            )
        up_near[step] = remote(
            pair_of(first, step), pair_of(down_first, step), up_send.at[step], up_recv.at[step], me, row - 1
        )
        down_near[step] = remote(
            pair_of(first, step), pair_of(up_first, step), down_send.at[step], down_recv.at[step], me, row + 1
        )
        up_far[step] = remote(
            pair_of(outgoing_first, step), pair_of(down_first, step), up_send.at[step], up_recv.at[step],
            target, row - 1,
        )
        down_far[step] = remote(
            pair_of(outgoing_first, step), pair_of(up_first, step), down_send.at[step], down_recv.at[step],
            target, row + 1,
        )

    def forward(step):
        @pl.when(near_up)
        def _():
            up_near[step].start()

        @pl.when(near_down)
        def _():
            down_near[step].start()

    for step in ORDER:
        label_copies[step].start()
    order = (0,) + ORDER
    for step in order[1 : WINDOW + 1]:
        frame_copies[step].start()

    for across, row_step in ((far_up, -1), (far_down, 1)):

        @pl.when(jnp.logical_and(across, ends))
        def _():
            pl.semaphore_signal(
                gate_sem, inc=1, device_id=(N_TM - 1 - me, row + row_step), device_id_type=MESH
            )

    @pl.when(jnp.logical_and(far, ends))
    def _():
        pl.semaphore_wait(gate_sem, 1)
        for distance in range(1, N_TM // 2):
            target = jnp.where(me == 0, me + distance, me - distance)
            pl.semaphore_signal(line_sem, inc=1, device_id=(target, row), device_id_type=MESH)

    forward(0)

    @pl.when(jnp.logical_not(has_up))
    def _():
        up_first[...] = jnp.zeros_like(up_first)

    @pl.when(jnp.logical_not(has_down))
    def _():
        down_first[...] = jnp.zeros_like(down_first)

    @pl.when(jnp.logical_not(has_before))
    def _():
        tail_before[...] = jnp.zeros_like(tail_before)
        second_before[...] = jnp.zeros_like(second_before)

    opened = []
    for span in range(2):
        start, hit = jnp.int32(0), jnp.bool_(False)
        for shot in range(4):
            hit = jnp.logical_or(hit, start == 2 * me + span)
            start = start + spans[shot]
        opened.append(hit)

    def find_places():
        for step in ORDER:
            label_copies[step].wait_recv()
        to_scalars = pltpu.make_async_copy(labels, labels_s, label_sem)
        to_scalars.start()
        to_scalars.wait()

        def scan_source(step, places):
            count = jnp.int32(0)
            for slot in range(F):
                held = labels_s[step, slot]
                mine = lax.shift_right_logical(held, 3) == me
                local = jnp.bitwise_and(held, F - 1)
                at = 2 * step + jnp.minimum(count, 1)
                places = tuple(jnp.where(jnp.logical_and(mine, local == f), at, places[f]) for f in range(F))
                count = count + mine.astype(jnp.int32)
            return places

        return lax.fori_loop(0, N_TM, scan_source, (jnp.int32(0),) * F)

    def take_in(step):
        frame_copies[step].wait_recv()
        for rank in range(2):
            for line in range(2):
                span_of = slice(line * PACK, (line + 1) * PACK)
                first[2 * step + rank, span_of] = norm_packed(
                    arrived[2 * step + rank, span_of], gain_low, gain_pairs
                )
        forward(step)

    def wait_halo(step):
        for has_side, copies in ((has_down, up_near), (has_up, down_near)):

            @pl.when(has_side)
            def _():
                copies[step].wait_recv()

    def convolve_pair(at, slots_of):
        for k in range(2):
            for source, base in ((first, 2), (up_first, 0), (down_first, 4)):
                block = source[slots_of[k]]
                for line in range(2):
                    grid_one[at + k, base + line] = spread(block[line * PACK : (line + 1) * PACK])
        for time_tap in range(3):
            share = conv(grid_one, at, 2, 4, w_one, (time_tap,))
            parts[time_tap, at : at + 2] = share.reshape(2, 4, COLS, CH)

    def convolve(step):
        convolve_pair(2 * step, (2 * step, 2 * step + 1))

    def lay_video(source, base):
        for f in range(F):
            block = source[places[f]]
            for line in range(2):
                grid_one[f, base + line] = spread(block[line * PACK : (line + 1) * PACK])

    def convolve_half(f, first_row):
        for time_tap in range(3):
            share = conv(grid_one, f, SPAN, 2, w_one, (time_tap,), first_row)
            parts[time_tap, f : f + SPAN, pl.ds(first_row, 2)] = share.reshape(SPAN, 2, COLS, CH)

    def wait_all(there, copies):
        @pl.when(there)
        def _():
            for step in order:
                copies[step].wait_recv()

    near_rows = jnp.where(far_down, 0, 2)
    far_rows = 2 - near_rows

    for i in range(1, N_TM):
        take_in(order[i])
        if i + WINDOW < N_TM:
            frame_copies[order[i]].wait_send()
            frame_copies[order[i + WINDOW]].start()
        if i == 1:

            @pl.when(jnp.logical_and(far, jnp.logical_not(ends)))
            def _():
                pl.semaphore_wait(line_sem, 1)

            for across, copies in ((far_up, up_far), (far_down, down_far)):

                @pl.when(across)
                def _():
                    for step in order:
                        copies[step].start()

        if i == 2:
            loads[5].wait()
            places = find_places()
        if i >= 2:

            @pl.when(jnp.logical_not(far))
            def _():
                wait_halo(order[i - 2])
                convolve(order[i - 2])

    def tail_copy(side):
        return remote(tail.at[side], tail_before.at[side], t_send.at[side], t_recv.at[side], me + 1, row)

    for k in range(2):
        tail[0, k] = first[places[F - 2 + k]]

    @pl.when(has_next)
    def _():
        tail_copy(0).start()

    @pl.when(jnp.logical_not(far))
    def _():
        wait_halo(order[-2])
        convolve(order[-2])
        wait_halo(order[-1])

    @pl.when(far)
    def _():
        lay_video(first, 2)
        wait_all(jnp.logical_and(far_down, has_up), down_near)
        wait_all(jnp.logical_and(far_up, has_down), up_near)
        pl.when(far_down)(functools.partial(lay_video, up_first, 0))
        pl.when(far_up)(functools.partial(lay_video, down_first, 4))
        convolve_half(SPAN, near_rows)
        convolve_half(0, near_rows)
        wait_all(far_down, up_near)
        wait_all(far_up, down_near)
        pl.when(far_down)(functools.partial(lay_video, down_first, 4))
        pl.when(far_up)(functools.partial(lay_video, up_first, 0))

    for k in range(2):
        tail[1, k] = up_first[places[F - 2 + k]]
        tail[2, k] = down_first[places[F - 2 + k]]

    @pl.when(has_next)
    def _():
        tail_copy(1).start()
        tail_copy(2).start()

    @pl.when(jnp.logical_not(far))
    def _():
        convolve(order[-1])

    @pl.when(far)
    def _():
        convolve_half(SPAN, far_rows)

    spots = [jnp.where(far, f, places[f]) for f in range(F)]
    for load in loads[2:5]:
        load.wait()

    line_of = lax.broadcasted_iota(jnp.int32, (2 * 4 * COLS, 1), 0) // COLS % 4
    outside = jnp.logical_or(
        jnp.logical_and(line_of == 0, jnp.logical_not(has_up)),
        jnp.logical_and(line_of == 3, jnp.logical_not(has_down)),
    )

    def part(time_tap, f):
        return parts[time_tap, spots[f]].reshape(4 * COLS, CH)

    def cut(span, share):
        return jnp.where(opened[span], jnp.zeros_like(share), share)

    def second_of(at, hidden):
        hidden = jnp.concatenate(hidden, axis=0) + bias_one[...]
        mean = jnp.sum(hidden * hidden, axis=-1, keepdims=True) * (1.0 / CH)
        second = silu(hidden * lax.rsqrt(mean + 1e-06) * gain_two[...])
        second = jnp.where(outside, 0.0, second).astype(BF16).reshape(2, 4, COLS, CH)
        grid_two[at : at + 2] = second
        return second

    def whole(f):
        return part(2, f) + part(1, f - 1) + part(0, f - 2)

    def finish(span):
        branch = conv(grid_two, 6 * span, SPAN, 2, w_two, (0, 1, 2)) + bias_two[...]
        for f in range(SPAN):
            block = arrived[places[SPAN * span + f]]
            for line in range(2):
                held = spread(block[line * PACK : (line + 1) * PACK]).astype(F32)
                at = (2 * f + line) * COLS
                out[SPAN * span + f, line] = (held + branch[at : at + COLS]).astype(BF16)

    second = second_of(10, [whole(6), whole(7)])
    for k in range(2):
        for line in range(4):
            second_tail[k, line * PACK : (line + 1) * PACK] = gathered(second[k, line])
    send_second = remote(second_tail, second_before, s_send, s_recv, me + 1, row)

    @pl.when(has_next)
    def _():
        send_second.start()

    @pl.when(far)
    def _():
        convolve_half(0, far_rows)

    second_of(8, [
        part(2, 4) + cut(1, part(1, 3) + part(0, 2)),
        part(2, 5) + part(1, 4) + cut(1, part(0, 3)),
    ])
    second = second_of(4, [whole(2), whole(3)])
    grid_two[6:8] = jnp.where(opened[1], jnp.zeros_like(second), second)
    loads[6].wait()
    finish(1)

    @pl.when(has_before)
    def _():
        for side in range(3):
            tail_copy(side).wait_recv()

    for side, base in ((0, 2), (1, 0), (2, 4)):
        for k in range(2):
            for line in range(2):
                grid_tail[k, base + line] = spread(tail_before[side, k, line * PACK : (line + 1) * PACK])
    two_back = conv(grid_tail, 0, 2, 4, w_one, (0,))
    one_back = conv(grid_tail, 1, 1, 4, w_one, (1,))
    second_of(2, [
        part(2, 0) + cut(0, one_back + two_back[: 4 * COLS]),
        part(2, 1) + part(1, 0) + cut(0, two_back[4 * COLS :]),
    ])

    @pl.when(has_before)
    def _():
        send_second.wait_recv()

    for k in range(2):
        for line in range(4):
            value = spread(second_before[k, line * PACK : (line + 1) * PACK])
            grid_two[k, line] = jnp.where(opened[0], jnp.zeros_like(value), value)
    finish(0)

    for step in ORDER:
        label_copies[step].wait_send()
    for step in order[N_TM - WINDOW :]:
        frame_copies[step].wait_send()
    for has_side, copies in ((has_up, up_near), (has_down, down_near)):

        @pl.when(has_side)
        def _():
            for step in order:
                copies[step].wait_send()

    @pl.when(has_next)
    def _():
        for side in range(3):
            tail_copy(side).wait_send()
        send_second.wait_send()


def body(
    frames_in, slot_frame, shot_spans, gain_one, conv_one, bias_one, gain_two, conv_two, bias_two
):
    vmem, smem, dma = pltpu.VMEM, pltpu.SMEM, pltpu.SemaphoreType.DMA
    whole = pl.BlockSpec(memory_space=vmem)
    hbm, scalars = pl.BlockSpec(memory_space=pltpu.HBM), pl.BlockSpec(memory_space=smem)
    taps, vector = (27, CH, CH), (1, CH)
    blocks = vmem((2 * N_TM, 2 * PACK, 128), BF16)
    return pl.pallas_call(
        functools.partial(kernel, lax.axis_size("rows")),
        out_shape=jax.ShapeDtypeStruct(frames_in.shape, BF16),
        in_specs=[hbm, scalars, scalars] + [hbm] * 6,
        out_specs=whole,
        scratch_shapes=[
            vmem(frames_in.shape, BF16),
            vmem(vector, F32),
            vmem(taps, BF16),
            vmem(vector, F32),
            vmem(vector, F32),
            vmem(taps, BF16),
            vmem(vector, F32),
            vmem((F, 2 * PACK, 128), BF16),
            vmem((F, 2 * PACK, 128), BF16),
            blocks, blocks, blocks, blocks, blocks, blocks,
            vmem((N_TM, 128), jnp.int32),
            smem((N_TM, 128), jnp.int32),
            vmem((3, 2, 2 * PACK, 128), BF16),
            vmem((3, 2, 2 * PACK, 128), BF16),
            vmem((2, 4 * PACK, 128), BF16),
            vmem((2, 4 * PACK, 128), BF16),
            vmem((2 * N_TM, 6, COLS, CH), BF16),
            vmem((2, 6, COLS, CH), BF16),
            vmem((3, 2 * N_TM, 4, COLS, CH), F32),
            vmem((12, 4, COLS, CH), BF16),
            dma((7,)),
            dma,
            dma((N_TM,)), dma((N_TM,)),
            dma((N_TM,)), dma((N_TM,)),
            dma((N_TM,)), dma((N_TM,)),
            dma((N_TM,)), dma((N_TM,)),
            dma((3,)), dma((3,)),
            dma, dma,
            pltpu.SemaphoreType.REGULAR, pltpu.SemaphoreType.REGULAR,
        ],
        name="residual_block",
        compiler_params=pltpu.CompilerParams(
            collective_id=1, has_side_effects=True, vmem_limit_bytes=60 << 20
        ),
    )(
        frames_in, slot_frame, shot_spans, gain_one.reshape(vector),
        conv_one.reshape(taps), bias_one.reshape(vector), gain_two.reshape(vector),
        conv_two.reshape(taps), bias_two.reshape(vector),
    )


def solution(mesh):
    placed = (P("tm", "rows", None, None), P("tm"), P(), P(), P(), P(), P(), P(), P())
    return jax.shard_map(
        body, mesh=mesh, in_specs=placed, out_specs=P("tm", "rows", None, None), check_vma=False
    )
```

```python
import functools

import jax
import jax.numpy as jnp
from jax import lax
from jax.experimental import pallas as pl
from jax.experimental.pallas import tpu as pltpu
from jax.sharding import PartitionSpec as P

SPAN = 4
CH = 192
COLS = 32
N_TM = 8
F = 8
PACK = 48
ORDER = (1, 7, 2, 6, 3, 5, 4)
WINDOW = 5
F32 = jnp.float32
BF16 = jnp.bfloat16
MESH = pl.DeviceIdType.MESH


def remote(src, dst, send, recv, tm, rows):
    return pltpu.make_async_remote_copy(
        src_ref=src, dst_ref=dst, send_sem=send, recv_sem=recv, device_id=(tm, rows), device_id_type=MESH
    )


def silu(u):
    return u / (1.0 + jnp.exp(-u))


def spread(packed):
    low, pairs = packed[:COLS], packed[COLS:]
    high = jnp.concatenate([pairs[:, :64], pairs[:, 64:]], axis=0)
    return jnp.concatenate([low, high], axis=1)


def gathered(image_row):
    high = image_row[:, 128:]
    pairs = jnp.concatenate([high[:16], high[16:]], axis=1)
    return jnp.concatenate([image_row[:, :128], pairs], axis=0)


def norm_packed(packed, gain_low, gain_pairs):
    values = packed.astype(F32)
    low, pairs = values[:COLS], values[COLS:]
    left = lax.broadcasted_iota(jnp.int32, pairs.shape, 1) < 64
    low_sum = jnp.sum(low * low, axis=-1, keepdims=True)
    squares = pairs * pairs
    left_sum = jnp.sum(jnp.where(left, squares, 0.0), axis=-1, keepdims=True)
    right_sum = jnp.sum(jnp.where(left, 0.0, squares), axis=-1, keepdims=True)
    total = low_sum + jnp.concatenate([left_sum, right_sum], axis=0)
    scale = lax.rsqrt(total * (1.0 / CH) + 1e-06)
    low_out = silu(low * scale * gain_low)
    pairs_out = silu(pairs * jnp.where(left, scale[:16], scale[16:]) * gain_pairs)
    return jnp.concatenate([low_out.astype(BF16), pairs_out.astype(BF16)], axis=0)


def col_taps(left, middle, right):
    count = middle.shape[0]
    col = lax.broadcasted_iota(jnp.int32, middle.shape, 0) % COLS
    from_left = jnp.where(col == 0, 0.0, pltpu.roll(left, 1, 0))
    from_right = jnp.where(col == COLS - 1, 0.0, pltpu.roll(right, count - 1, 0))
    return middle + from_left + from_right


def conv(source, base, frames, rows, weight, time_taps, first_row=0):
    count = frames * rows * COLS
    sums = [jnp.zeros((count, CH), F32) for _ in range(3)]
    for time_tap in time_taps:
        at = base if len(time_taps) == 1 else base + time_tap
        for row_tap in range(3):
            tile = source[pl.ds(at, frames), pl.ds(first_row + row_tap, rows)].reshape(count, CH)
            for col_tap in range(3):
                tap = weight[(time_tap * 3 + row_tap) * 3 + col_tap]
                sums[col_tap] = sums[col_tap] + jnp.dot(tile, tap, preferred_element_type=F32)
    return col_taps(*sums)


def kernel(
    n_rows,
    frames_h, slots, spans, gain_one_h, conv_one_h, bias_one_h, gain_two_h, conv_two_h, bias_two_h,
    out,
    frames, gain_one, w_one, bias_one, gain_two, w_two, bias_two,
    packed, packed_first, outgoing, outgoing_first, arrived, first, up_first, down_first,
    labels, labels_s, tail, tail_before, second_tail, second_before, grid_one, grid_tail, parts, grid_two,
    in_sem, label_sem, l_send, l_recv, a_send, a_recv, up_send, up_recv, down_send, down_recv,
    t_send, t_recv, s_send, s_recv, gate_sem, line_sem,
):
    me = lax.axis_index("tm")
    row = lax.axis_index("rows")
    has_up, has_down = row > 0, row < n_rows - 1
    has_next, has_before = me < N_TM - 1, me > 0
    far_up, far_down = row == n_rows // 2, row == n_rows // 2 - 1
    far = jnp.logical_or(far_up, far_down)
    ends = jnp.logical_or(me == 0, me == N_TM - 1)
    near_up = jnp.logical_and(has_up, jnp.logical_not(far_up))
    near_down = jnp.logical_and(has_down, jnp.logical_not(far_down))

    barrier = pltpu.get_barrier_semaphore()
    peers = jnp.int32(N_TM - 1)
    for near, across, row_step in ((near_up, far_up, -1), (near_down, far_down, 1)):
        greets = jnp.logical_and(across, ends)
        peers = peers + near.astype(jnp.int32) + greets.astype(jnp.int32)

        @pl.when(near)
        def _():
            pl.semaphore_signal(barrier, inc=1, device_id=(me, row + row_step), device_id_type=MESH)

        @pl.when(greets)
        def _():
            pl.semaphore_signal(
                barrier, inc=1, device_id=(N_TM - 1 - me, row + row_step), device_id_type=MESH
            )

    for step in ORDER:
        pl.semaphore_signal(barrier, inc=1, device_id=(lax.rem(me + step, N_TM), row), device_id_type=MESH)

    loads = [
        pltpu.make_async_copy(src, dst, in_sem.at[i])
        for i, (src, dst) in enumerate((
            (frames_h, frames), (gain_one_h, gain_one), (bias_one_h, bias_one), (gain_two_h, gain_two),
            (bias_two_h, bias_two), (conv_one_h, w_one), (conv_two_h, w_two),
        ))
    ]
    for load in loads:
        load.start()

    lane = lax.broadcasted_iota(jnp.int32, (1, 128), 1)
    held = jnp.zeros((1, 128), jnp.int32)
    for slot in range(F):
        held = jnp.where(lane == slot, slots[slot], held)
    labels[0:1] = held

    loads[0].wait()
    loads[1].wait()
    gain = gain_one[...]
    gain_low = gain[:, :128]
    gain_pairs = jnp.concatenate([gain[:, 128:], gain[:, 128:]], axis=1)
    for slot in range(F):
        for line in range(2):
            span_of = slice(line * PACK, (line + 1) * PACK)
            block = gathered(frames[slot, line])
            packed[slot, span_of] = block
            packed_first[slot, span_of] = norm_packed(block, gain_low, gain_pairs)
    for step in range(N_TM):
        target = lax.rem(me + step, N_TM)
        count = jnp.int32(0)
        picks = [jnp.int32(0), jnp.int32(0)]
        for slot in range(F):
            mine = lax.shift_right_logical(slots[slot], 3) == target
            for rank in range(2):
                picks[rank] = jnp.where(jnp.logical_and(mine, count == rank), slot, picks[rank])
            count = count + mine.astype(jnp.int32)
        for rank in range(2):
            at = 2 * step + rank
            outgoing_first[at] = packed_first[picks[rank]]
            if step:
                outgoing[at] = packed[picks[rank]]
            else:
                arrived[rank] = packed[picks[rank]]
                first[rank] = packed_first[picks[rank]]

    pl.semaphore_wait(barrier, peers)

    def pair_of(ref, step):
        return ref.at[pl.ds(2 * step, 2)]

    label_copies, frame_copies, up_near, up_far, down_near, down_far = {}, {}, {}, {}, {}, {}
    for step in range(N_TM):
        target = lax.rem(me + step, N_TM)
        if step:
            label_copies[step] = remote(
                labels.at[pl.ds(0, 1)], labels.at[pl.ds(step, 1)], l_send.at[step], l_recv.at[step], target, row
            )
            frame_copies[step] = remote(
                pair_of(outgoing, step), pair_of(arrived, step), a_send.at[step], a_recv.at[step], target, row
            )
        up_near[step] = remote(
            pair_of(first, step), pair_of(down_first, step), up_send.at[step], up_recv.at[step], me, row - 1
        )
        down_near[step] = remote(
            pair_of(first, step), pair_of(up_first, step), down_send.at[step], down_recv.at[step], me, row + 1
        )
        up_far[step] = remote(
            pair_of(outgoing_first, step), pair_of(down_first, step), up_send.at[step], up_recv.at[step],
            target, row - 1,
        )
        down_far[step] = remote(
            pair_of(outgoing_first, step), pair_of(up_first, step), down_send.at[step], down_recv.at[step],
            target, row + 1,
        )

    def forward(step):
        @pl.when(near_up)
        def _():
            up_near[step].start()

        @pl.when(near_down)
        def _():
            down_near[step].start()

    for step in ORDER:
        label_copies[step].start()
    order = (0,) + ORDER
    for step in order[1 : WINDOW + 1]:
        frame_copies[step].start()

    for across, row_step in ((far_up, -1), (far_down, 1)):

        @pl.when(jnp.logical_and(across, ends))
        def _():
            pl.semaphore_signal(
                gate_sem, inc=1, device_id=(N_TM - 1 - me, row + row_step), device_id_type=MESH
            )

    @pl.when(jnp.logical_and(far, ends))
    def _():
        pl.semaphore_wait(gate_sem, 1)
        for distance in range(1, N_TM // 2):
            target = jnp.where(me == 0, me + distance, me - distance)
            pl.semaphore_signal(line_sem, inc=1, device_id=(target, row), device_id_type=MESH)

    forward(0)

    @pl.when(jnp.logical_not(has_up))
    def _():
        up_first[...] = jnp.zeros_like(up_first)

    @pl.when(jnp.logical_not(has_down))
    def _():
        down_first[...] = jnp.zeros_like(down_first)

    @pl.when(jnp.logical_not(has_before))
    def _():
        tail_before[...] = jnp.zeros_like(tail_before)
        second_before[...] = jnp.zeros_like(second_before)

    opened = []
    for span in range(2):
        start, hit = jnp.int32(0), jnp.bool_(False)
        for shot in range(4):
            hit = jnp.logical_or(hit, start == 2 * me + span)
            start = start + spans[shot]
        opened.append(hit)

    def find_places():
        for step in ORDER:
            label_copies[step].wait_recv()
        to_scalars = pltpu.make_async_copy(labels, labels_s, label_sem)
        to_scalars.start()
        to_scalars.wait()

        def scan_source(step, places):
            count = jnp.int32(0)
            for slot in range(F):
                held = labels_s[step, slot]
                mine = lax.shift_right_logical(held, 3) == me
                local = jnp.bitwise_and(held, F - 1)
                at = 2 * step + jnp.minimum(count, 1)
                places = tuple(jnp.where(jnp.logical_and(mine, local == f), at, places[f]) for f in range(F))
                count = count + mine.astype(jnp.int32)
            return places

        return lax.fori_loop(0, N_TM, scan_source, (jnp.int32(0),) * F)

    def take_in(step):
        frame_copies[step].wait_recv()
        for rank in range(2):
            for line in range(2):
                span_of = slice(line * PACK, (line + 1) * PACK)
                first[2 * step + rank, span_of] = norm_packed(
                    arrived[2 * step + rank, span_of], gain_low, gain_pairs
                )
        forward(step)

    def wait_halo(step):
        for has_side, copies in ((has_down, up_near), (has_up, down_near)):

            @pl.when(has_side)
            def _():
                copies[step].wait_recv()

    def convolve_pair(at, slots_of):
        for k in range(2):
            for source, base in ((first, 2), (up_first, 0), (down_first, 4)):
                block = source[slots_of[k]]
                for line in range(2):
                    grid_one[at + k, base + line] = spread(block[line * PACK : (line + 1) * PACK])
        for time_tap in range(3):
            share = conv(grid_one, at, 2, 4, w_one, (time_tap,))
            parts[time_tap, at : at + 2] = share.reshape(2, 4, COLS, CH)

    def convolve(step):
        convolve_pair(2 * step, (2 * step, 2 * step + 1))

    def lay_video(source, base):
        for f in range(F):
            block = source[places[f]]
            for line in range(2):
                grid_one[f, base + line] = spread(block[line * PACK : (line + 1) * PACK])

    def convolve_half(f, first_row):
        for time_tap in range(3):
            share = conv(grid_one, f, SPAN, 2, w_one, (time_tap,), first_row)
            parts[time_tap, f : f + SPAN, pl.ds(first_row, 2)] = share.reshape(SPAN, 2, COLS, CH)

    def wait_all(there, copies):
        @pl.when(there)
        def _():
            for step in order:
                copies[step].wait_recv()

    near_rows = jnp.where(far_down, 0, 2)
    far_rows = 2 - near_rows

    for i in range(1, N_TM):
        take_in(order[i])
        if i + WINDOW < N_TM:
            frame_copies[order[i]].wait_send()
            frame_copies[order[i + WINDOW]].start()
        if i == 1:

            @pl.when(jnp.logical_and(far, jnp.logical_not(ends)))
            def _():
                pl.semaphore_wait(line_sem, 1)

            for across, copies in ((far_up, up_far), (far_down, down_far)):

                @pl.when(across)
                def _():
                    for step in order:
                        copies[step].start()

        if i == 2:
            loads[5].wait()
            places = find_places()
        if i >= 2:

            @pl.when(jnp.logical_not(far))
            def _():
                wait_halo(order[i - 2])
                convolve(order[i - 2])

    def tail_copy(side):
        return remote(tail.at[side], tail_before.at[side], t_send.at[side], t_recv.at[side], me + 1, row)

    for k in range(2):
        tail[0, k] = first[places[F - 2 + k]]

    @pl.when(has_next)
    def _():
        tail_copy(0).start()

    @pl.when(jnp.logical_not(far))
    def _():
        wait_halo(order[-2])
        convolve(order[-2])
        wait_halo(order[-1])

    @pl.when(far)
    def _():
        lay_video(first, 2)
        wait_all(jnp.logical_and(far_down, has_up), down_near)
        wait_all(jnp.logical_and(far_up, has_down), up_near)
        pl.when(far_down)(functools.partial(lay_video, up_first, 0))
        pl.when(far_up)(functools.partial(lay_video, down_first, 4))
        convolve_half(SPAN, near_rows)
        convolve_half(0, near_rows)
        wait_all(far_down, up_near)
        wait_all(far_up, down_near)
        pl.when(far_down)(functools.partial(lay_video, down_first, 4))
        pl.when(far_up)(functools.partial(lay_video, up_first, 0))

    for k in range(2):
        tail[1, k] = up_first[places[F - 2 + k]]
        tail[2, k] = down_first[places[F - 2 + k]]

    @pl.when(has_next)
    def _():
        tail_copy(1).start()
        tail_copy(2).start()

    @pl.when(jnp.logical_not(far))
    def _():
        convolve(order[-1])

    @pl.when(far)
    def _():
        convolve_half(SPAN, far_rows)

    spots = [jnp.where(far, f, places[f]) for f in range(F)]
    for load in loads[2:5]:
        load.wait()

    line_of = lax.broadcasted_iota(jnp.int32, (2 * 4 * COLS, 1), 0) // COLS % 4
    outside = jnp.logical_or(
        jnp.logical_and(line_of == 0, jnp.logical_not(has_up)),
        jnp.logical_and(line_of == 3, jnp.logical_not(has_down)),
    )

    def part(time_tap, f):
        return parts[time_tap, spots[f]].reshape(4 * COLS, CH)

    def cut(span, share):
        return jnp.where(opened[span], jnp.zeros_like(share), share)

    def second_of(at, hidden):
        hidden = jnp.concatenate(hidden, axis=0) + bias_one[...]
        mean = jnp.sum(hidden * hidden, axis=-1, keepdims=True) * (1.0 / CH)
        second = silu(hidden * lax.rsqrt(mean + 1e-06) * gain_two[...])
        second = jnp.where(outside, 0.0, second).astype(BF16).reshape(2, 4, COLS, CH)
        grid_two[at : at + 2] = second
        return second

    def whole(f):
        return part(2, f) + part(1, f - 1) + part(0, f - 2)

    def finish(span):
        branch = conv(grid_two, 6 * span, SPAN, 2, w_two, (0, 1, 2)) + bias_two[...]
        for f in range(SPAN):
            block = arrived[places[SPAN * span + f]]
            for line in range(2):
                held = spread(block[line * PACK : (line + 1) * PACK]).astype(F32)
                at = (2 * f + line) * COLS
                out[SPAN * span + f, line] = (held + branch[at : at + COLS]).astype(BF16)

    second = second_of(10, [whole(6), whole(7)])
    for k in range(2):
        for line in range(4):
            second_tail[k, line * PACK : (line + 1) * PACK] = gathered(second[k, line])
    send_second = remote(second_tail, second_before, s_send, s_recv, me + 1, row)

    @pl.when(has_next)
    def _():
        send_second.start()

    @pl.when(far)
    def _():
        convolve_half(0, far_rows)

    second_of(8, [
        part(2, 4) + cut(1, part(1, 3) + part(0, 2)),
        part(2, 5) + part(1, 4) + cut(1, part(0, 3)),
    ])
    second = second_of(4, [whole(2), whole(3)])
    grid_two[6:8] = jnp.where(opened[1], jnp.zeros_like(second), second)
    loads[6].wait()
    finish(1)

    @pl.when(has_before)
    def _():
        for side in range(3):
            tail_copy(side).wait_recv()

    for side, base in ((0, 2), (1, 0), (2, 4)):
        for k in range(2):
            for line in range(2):
                grid_tail[k, base + line] = spread(tail_before[side, k, line * PACK : (line + 1) * PACK])
    two_back = conv(grid_tail, 0, 2, 4, w_one, (0,))
    one_back = conv(grid_tail, 1, 1, 4, w_one, (1,))
    second_of(2, [
        part(2, 0) + cut(0, one_back + two_back[: 4 * COLS]),
        part(2, 1) + part(1, 0) + cut(0, two_back[4 * COLS :]),
    ])

    @pl.when(has_before)
    def _():
        send_second.wait_recv()

    for k in range(2):
        for line in range(4):
            value = spread(second_before[k, line * PACK : (line + 1) * PACK])
            grid_two[k, line] = jnp.where(opened[0], jnp.zeros_like(value), value)
    finish(0)

    for step in ORDER:
        label_copies[step].wait_send()
    for step in order[N_TM - WINDOW :]:
        frame_copies[step].wait_send()
    for has_side, copies in ((has_up, up_near), (has_down, down_near)):

        @pl.when(has_side)
        def _():
            for step in order:
                copies[step].wait_send()

    @pl.when(has_next)
    def _():
        for side in range(3):
            tail_copy(side).wait_send()
        send_second.wait_send()


def body(
    frames_in, slot_frame, shot_spans, gain_one, conv_one, bias_one, gain_two, conv_two, bias_two
):
    vmem, smem, dma = pltpu.VMEM, pltpu.SMEM, pltpu.SemaphoreType.DMA
    whole = pl.BlockSpec(memory_space=vmem)
    hbm, scalars = pl.BlockSpec(memory_space=pltpu.HBM), pl.BlockSpec(memory_space=smem)
    taps, vector = (27, CH, CH), (1, CH)
    blocks = vmem((2 * N_TM, 2 * PACK, 128), BF16)
    return pl.pallas_call(
        functools.partial(kernel, lax.axis_size("rows")),
        out_shape=jax.ShapeDtypeStruct(frames_in.shape, BF16),
        in_specs=[hbm, scalars, scalars] + [hbm] * 6,
        out_specs=whole,
        scratch_shapes=[
            vmem(frames_in.shape, BF16),
            vmem(vector, F32),
            vmem(taps, BF16),
            vmem(vector, F32),
            vmem(vector, F32),
            vmem(taps, BF16),
            vmem(vector, F32),
            vmem((F, 2 * PACK, 128), BF16),
            vmem((F, 2 * PACK, 128), BF16),
            blocks, blocks, blocks, blocks, blocks, blocks,
            vmem((N_TM, 128), jnp.int32),
            smem((N_TM, 128), jnp.int32),
            vmem((3, 2, 2 * PACK, 128), BF16),
            vmem((3, 2, 2 * PACK, 128), BF16),
            vmem((2, 4 * PACK, 128), BF16),
            vmem((2, 4 * PACK, 128), BF16),
            vmem((2 * N_TM, 6, COLS, CH), BF16),
            vmem((2, 6, COLS, CH), BF16),
            vmem((3, 2 * N_TM, 4, COLS, CH), F32),
            vmem((12, 4, COLS, CH), BF16),
            dma((7,)),
            dma,
            dma((N_TM,)), dma((N_TM,)),
            dma((N_TM,)), dma((N_TM,)),
            dma((N_TM,)), dma((N_TM,)),
            dma((N_TM,)), dma((N_TM,)),
            dma((3,)), dma((3,)),
            dma, dma,
            pltpu.SemaphoreType.REGULAR, pltpu.SemaphoreType.REGULAR,
        ],
        name="residual_block",
        compiler_params=pltpu.CompilerParams(
            collective_id=1, has_side_effects=True, vmem_limit_bytes=60 << 20
        ),
    )(
        frames_in, slot_frame, shot_spans, gain_one.reshape(vector),
        conv_one.reshape(taps), bias_one.reshape(vector), gain_two.reshape(vector),
        conv_two.reshape(taps), bias_two.reshape(vector),
    )


def solution(mesh):
    placed = (P("tm", "rows", None, None), P("tm"), P(), P(), P(), P(), P(), P(), P())
    return jax.shard_map(
        body, mesh=mesh, in_specs=placed, out_specs=P("tm", "rows", None, None), check_vma=False
    )
```
